512 devices in a mesh: inst: 8 (over y, core), space: 64 (over x, z).
Axes of the slice: x: 4, y: 4, z: 16, core: 2. Of those that a mesh axis runs over, the one named last changes fastest.
Arguments:
- amplitudes: float32 [8, 40], replicated, may hold values from -6 to 6
- modal_coeffs: float32 [40, 3, 4096], P(None, None, ('inst', 'space')), may hold values from -0.6 to 0.6
- centre_positions: float32 [3, 4096], P(None, ('inst', 'space')), may hold values from 0 to 256
- base_nodes: float32 [3, 128, 64, 256], P(None, 'space'), may hold values from -1 to 256
Outputs:
- displacement: float32 [8, 3, 128, 64, 256], P('inst', None, 'space')
- metrics: float32 [8, 10, 128, 64, 256], P('inst', None, 'space')
The draws below stay inside these ranges and needn't reach their ends.
All inputs are finite; a program needn't handle non-finite values.
Results may differ from the reference program's by a relative error of at most 0.0003.
Values sent between devices are 32-bit elements; how exact they have to be, the bound alone decides.
A program may use at most 64 MiB of HBM per device.

```python
import math
import jax
import jax.numpy as jnp
from jax import lax

M = 40
NC = 4096
NJ = 64
NK = 256
INST = 8
NI = 128


def draw_centre_positions(key, part):
    key = jax.random.fold_in(key, 11)
    unit = jax.random.uniform(jax.random.fold_in(key, 1), (3, NC), jnp.float32)
    pick = jax.random.uniform(jax.random.fold_in(key, 2), (NC,), jnp.float32)
    spot = jax.random.uniform(jax.random.fold_in(key, 3), (), jnp.float32)
    wing_share = 0.5
    band = 4.0
    wing_centre = 0.5 * band + spot * (NI - 1.0 - band)
    wing_i = wing_centre + (unit[0] - 0.5) * band
    wing_j = (NJ - 1.0) * unit[1]
    wing_k = (NK - 1.0) * unit[2]
    tube_i = (NI - 1.0) * unit[0]
    tube_j = 0.5 * (NJ - 1.0) + (unit[1] - 0.5) * min(8.0, NJ - 1.0)
    tube_k = 0.5 * (NK - 1.0) + (unit[2] - 0.5) * min(16.0, NK - 1.0)
    on_wing = pick < wing_share
    return jnp.stack([jnp.where(on_wing, wing_i, tube_i), jnp.where(on_wing, wing_j, tube_j), jnp.where(on_wing, wing_k, tube_k)], axis=0)


def draw_base_nodes(key, part):
    shape = (NI, NJ, NK)
    lattice = jnp.stack([lax.broadcasted_iota(jnp.float32, shape, 0), lax.broadcasted_iota(jnp.float32, shape, 1), lax.broadcasted_iota(jnp.float32, shape, 2)], axis=0)
    jitter = jax.random.uniform(key, (3, NI, NJ, NK), jnp.float32, -0.3, 0.3)
    return lattice + jitter


def steps_of(stream_key, dims, pieces, low, top_value):
    def one(dim, parts):
        draws = jax.random.uniform(jax.random.fold_in(jax.random.fold_in(stream_key, 6), dim), (parts,), jnp.float32, low / len(pieces), top_value / len(pieces))
        return jnp.repeat(jnp.exp(draws), dims[dim] // parts).reshape((-1,) + (1,) * (len(dims) - dim - 1))

    factor_of = one(*pieces[0])
    for cut in pieces[1:]:
        factor_of = factor_of * one(*cut)
    return factor_of


def noise(rng, dims, spread, limit, split=(), kind=jnp.bfloat16):
    factor_of = steps_of(rng, dims, split, -0.22, 0.18) if split else 1.0
    result = jax.random.normal(rng, dims, jnp.float32) * spread * factor_of
    return jnp.minimum(jnp.maximum(result, -limit), limit).astype(kind)


def setup_inputs(seed: int = 0) -> dict:
    arg_keys = jax.random.split(jax.random.key(seed), 5)
    return {
        "amplitudes": noise(arg_keys[0], (INST, M), 1.0, 6.0, (), jnp.float32),
        "modal_coeffs": noise(arg_keys[1], (M, 3, NC), 0.1, 0.6, ((2, 512),), jnp.float32),
        "centre_positions": draw_centre_positions(jax.random.fold_in(arg_keys[4], 71), 0),
        "base_nodes": draw_base_nodes(jax.random.fold_in(arg_keys[4], 71), 0),
    }


support = 4.0

def kernel_tile(centres, node_list):
    separation = centres[0][:, None] - node_list[0][None, :]
    square = separation * separation
    separation = centres[1][:, None] - node_list[1][None, :]
    square = square + separation * separation
    separation = centres[2][:, None] - node_list[2][None, :]
    square = square + separation * separation
    radius = jnp.sqrt(square) / support
    inside = jnp.maximum(1.0 - radius, 0.0)
    inside_sq = inside * inside
    return inside_sq * inside_sq * (4.0 * radius + 1.0)

def accumulate(running, centre_moves, centres, node_list):
    length = centres.shape[1]
    block_size = math.gcd(length, 512)
    turns = length // block_size

    def add_block(number, partial_value):
        begin_at = jnp.asarray(number, jnp.int32) * block_size
        piece_moves = lax.dynamic_slice_in_dim(centre_moves, begin_at, block_size, 1)
        piece_centres = lax.dynamic_slice_in_dim(centres, begin_at, block_size, 1)
        tile = kernel_tile(piece_centres, node_list)
        return partial_value + jnp.dot(piece_moves, tile, precision=lax.Precision.HIGHEST, preferred_element_type=jnp.float32)
    return lax.fori_loop(0, turns, add_block, running)

def central(values, which_dim):
    extent = values.shape[which_dim]
    head_row = lax.slice_in_dim(values, 0, 1, axis=which_dim)
    second = lax.slice_in_dim(values, 1, 2, axis=which_dim)
    tail_row = lax.slice_in_dim(values, extent - 1, extent, axis=which_dim)
    before = lax.slice_in_dim(values, extent - 2, extent - 1, axis=which_dim)
    extended = jnp.concatenate([2.0 * head_row - second, values, 2.0 * tail_row - before], axis=which_dim)
    upper_part = lax.slice_in_dim(extended, 2, extent + 2, axis=which_dim)
    lower_part = lax.slice_in_dim(extended, 0, extent, axis=which_dim)
    return (upper_part - lower_part) * 0.5

def cross_product(left_arm, right_arm):
    return jnp.stack([left_arm[:, 1] * right_arm[:, 2] - left_arm[:, 2] * right_arm[:, 1], left_arm[:, 2] * right_arm[:, 0] - left_arm[:, 0] * right_arm[:, 2], left_arm[:, 0] * right_arm[:, 1] - left_arm[:, 1] * right_arm[:, 0]], axis=1)

def metric_stack(along_i, along_j, along_k):
    first_vec = cross_product(along_j, along_k)
    second_vec = cross_product(along_k, along_i)
    third_vec = cross_product(along_i, along_j)
    jacobian = along_i[:, 0] * first_vec[:, 0] + along_i[:, 1] * first_vec[:, 1] + along_i[:, 2] * first_vec[:, 2]
    return jnp.concatenate([first_vec, second_vec, third_vec, jacobian[:, None]], axis=1)

def reference(amplitudes, modal_coeffs, centre_positions, base_nodes):
    centre_moves = jnp.einsum('tm,mcn->tcn', amplitudes, modal_coeffs, precision=lax.Precision.HIGHEST)
    centre_moves = centre_moves.reshape(INST * 3, NC)
    total_nodes = NI * NJ * NK
    block_size = math.gcd(total_nodes, 4096)
    turns = total_nodes // block_size
    stacked = base_nodes.reshape(3, turns, block_size).transpose(1, 0, 2)

    def one_block(chosen):
        start_value = jnp.zeros((INST * 3, block_size), jnp.float32)
        return accumulate(start_value, centre_moves, centre_positions, chosen)
    blocks = lax.map(one_block, stacked)
    displacement = blocks.transpose(1, 0, 2).reshape(INST, 3, NI, NJ, NK)
    deformed = base_nodes[None] + displacement
    along_i = central(deformed, 2)
    along_j = central(deformed, 3)
    along_k = central(deformed, 4)
    return (displacement, metric_stack(along_i, along_j, along_k))
```

```python
import jax
import jax.numpy as jnp
from jax import lax
from jax.experimental import pallas as pl
from jax.experimental.pallas import tpu as pltpu
from jax.sharding import PartitionSpec as P

MESH = pl.DeviceIdType.MESH
HIGH = lax.Precision.HIGHEST
XS, YS, ZS, CORES = 4, 4, 16, 2
INST, SPACE = YS * CORES, XS * ZS
OWN = 8
BLOCKS = XS * YS * CORES
NC = BLOCKS * ZS * OWN
VALUES = 32
BINS = 16
CHUNK = 128
PLACED = 256
MARGIN = 1.0 + 2.0**-11
VMEM_LIMIT = 48 * 1024 * 1024


def vmem():
    return pl.BlockSpec(memory_space=pltpu.VMEM)


def params(**more):
    return pltpu.CompilerParams(vmem_limit_bytes=VMEM_LIMIT, **more)


def gather_kernel(amp_ref, coef_ref, pos_ref, out_ref, zbuf, send, recv):
    inst, space = lax.axis_index("inst"), lax.axis_index("space")
    y, core = inst // CORES, inst % CORES
    x, z = space // ZS, space % ZS
    z_peers = [(inst, x * ZS + lax.rem(z + k, ZS)) for k in range(1, ZS)]
    x_peers = [(inst, lax.rem(x + k, XS) * ZS + z) for k in range(1, XS)]
    y_peers = [(lax.rem(y + k, YS) * CORES + core, space) for k in range(1, YS)]
    other = [(y * CORES + (1 - core), space)]
    peers = z_peers + x_peers + y_peers + other
    barrier = pltpu.get_barrier_semaphore()
    for peer in peers:
        pl.semaphore_signal(barrier, inc=1, device_id=peer, device_id_type=MESH)

    amp = amp_ref[...]
    rows = [
        jnp.dot(amp, coef_ref[:, c, :], precision=HIGH, preferred_element_type=jnp.float32)
        for c in range(3)
    ]
    rows += [pos_ref[...], jnp.zeros((5, OWN), jnp.float32)]
    own = jnp.concatenate(rows, axis=0)
    own = jnp.concatenate([own, jnp.zeros((VALUES, 128 - OWN), jnp.float32)], axis=1)
    own = jnp.concatenate([own, jnp.zeros((128 - VALUES, 128), jnp.float32)], axis=0)
    own = own.T[0:OWN]
    row_id = lax.broadcasted_iota(jnp.int32, (OWN, 128), 0) % 4
    spread = jnp.zeros((OWN, 128), jnp.float32)
    for a in range(4):
        moved = own if a == 0 else pltpu.roll(own, VALUES * a, 1)
        spread = spread + jnp.where(row_id == a, moved, 0.0)
    zbuf[z] = jnp.concatenate(
        [
            jnp.sum(spread[0:4], axis=0, keepdims=True),
            jnp.sum(spread[4:8], axis=0, keepdims=True),
        ],
        axis=0,
    )
    pl.semaphore_wait(barrier, len(peers))

    def send_all(ref, targets, first):
        copies = []
        for k, peer in enumerate(targets):
            copy = pltpu.make_async_remote_copy(
                src_ref=ref,
                dst_ref=ref,
                send_sem=send.at[first + k],
                recv_sem=recv.at[first + k],
                device_id=peer,
                device_id_type=MESH,
            )
            copy.start()
            copies.append(copy)
        return copies

    copies = send_all(zbuf.at[z], z_peers, 0)
    for copy in copies:
        copy.wait()
    rows = jnp.concatenate([zbuf[i] for i in range(ZS)], axis=0)
    rows = jnp.concatenate([rows, jnp.zeros((128 - 2 * ZS, 128), jnp.float32)], axis=0).T
    block = rows[0:VALUES]
    for a in range(1, 4):
        block = block + pltpu.roll(rows[VALUES * a : VALUES * (a + 1)], VALUES * a, 1)
    row = core * (XS * YS) + y * XS
    out_ref[row + x] = block
    copies = send_all(out_ref.at[row + x], x_peers, ZS - 1)
    for copy in copies:
        copy.wait()
    copies = send_all(out_ref.at[pl.ds(row, XS)], y_peers, ZS + XS - 2)
    for copy in copies:
        copy.wait()
    copies = send_all(out_ref.at[pl.ds(core * (XS * YS), XS * YS)], other, ZS + XS + YS - 3)
    for copy in copies:
        copy.wait()


def gather(amplitudes, coefficients, positions):
    count = ZS + XS + YS - 2
    return pl.pallas_call(
        gather_kernel,
        out_shape=jax.ShapeDtypeStruct((BLOCKS, VALUES, 128), jnp.float32),
        in_specs=[vmem()] * 3,
        out_specs=vmem(),
        scratch_shapes=[
            pltpu.VMEM((ZS, 2, 128), jnp.float32),
            pltpu.SemaphoreType.DMA((count,)),
            pltpu.SemaphoreType.DMA((count,)),
        ],
        compiler_params=params(collective_id=0, has_side_effects=True),
        name="gather",
    )(amplitudes, coefficients, positions)


def whole_dot(a, b, dims=(((1,), (0,)), ((), ()))):
    return lax.dot_general(a, b, dims, preferred_element_type=jnp.float32)


def evaluate_kernel(place, g_ref, n_ref, moved_ref, deformed_ref, nodes, parts, order, weights, centres, ends):
    strip = place()
    first = pl.multiple_of(strip * 8, 8)
    base = []
    for c in range(3):
        for p in range(2):
            value = n_ref[c, p, pl.ds(first, 8), :]
            base.append(value)
            nodes[c, p] = value * 0.25

    spots = [g_ref[:, 24 + c, :] * 0.25 for c in range(3)]
    near = None
    for c in range(3):
        low = jnp.min(nodes[c]) - MARGIN
        high = jnp.max(nodes[c]) + MARGIN
        inside = (spots[c] >= low) & (spots[c] <= high)
        near = inside if near is None else near & inside
        if c == 1:
            j_low, scale = low, BINS / jnp.full((1, 1), high - low)

    def bin_of(value):
        return jnp.clip(jnp.floor((value - j_low) * scale), 0.0, BINS - 1.0)

    bins = jnp.where(near, bin_of(spots[1]), -1.0)

    member = jnp.concatenate(
        [(bins == float(b)).astype(jnp.float32) for b in range(BINS)], axis=0
    )
    short = member.astype(jnp.bfloat16)
    size = BINS * BLOCKS

    def less(shape, shift):
        return (
            lax.broadcasted_iota(jnp.int32, shape, 0) + shift
            <= lax.broadcasted_iota(jnp.int32, shape, 1)
        ).astype(jnp.float32).astype(jnp.bfloat16)

    before = whole_dot(short, less((128, 128), 0))
    totals = whole_dot(short, jnp.ones((128, 128), jnp.bfloat16))
    earlier = (
        lax.broadcasted_iota(jnp.int32, (size, size), 1)
        < lax.broadcasted_iota(jnp.int32, (size, size), 0)
    ).astype(jnp.float32).astype(jnp.bfloat16)
    offsets = whole_dot(earlier, totals.astype(jnp.bfloat16))
    placed = member * (before + offsets)
    position = placed[0:BLOCKS]
    for b in range(1, BINS):
        position = position + placed[b * BLOCKS : (b + 1) * BLOCKS]
    position = position - 1.0
    for i in range(BLOCKS // 2):
        order[i : i + 1, 0:128] = position[2 * i : 2 * i + 1]
        order[i : i + 1, 128:256] = position[2 * i + 1 : 2 * i + 2]
    found = jnp.max(position).astype(jnp.int32) + 1

    row_low = jnp.min(jnp.min(nodes[1], axis=0), axis=1, keepdims=True)
    row_high = jnp.max(jnp.max(nodes[1], axis=0), axis=1, keepdims=True)
    row_low, row_high = bin_of(row_low - MARGIN), bin_of(row_high + MARGIN)
    for j in range(8):
        start = jnp.sum(((bins >= 0.0) & (bins < row_low[j : j + 1])).astype(jnp.float32))
        stop = jnp.sum(((bins >= 0.0) & (bins <= row_high[j : j + 1])).astype(jnp.float32))
        ends[0, j] = start.astype(jnp.int32) // CHUNK
        ends[1, j] = (stop.astype(jnp.int32) + (CHUNK - 1)) // CHUNK

    def split(i, carry):
        for half in range(2):
            value = g_ref[2 * i + half]
            motion = value[0:24]
            top = motion.astype(jnp.bfloat16).astype(jnp.float32)
            spot = value[24:32] * 0.25
            one = spot.astype(jnp.bfloat16).astype(jnp.float32)
            two = (spot - one).astype(jnp.bfloat16).astype(jnp.float32)
            three = spot - one - two
            parts[i, :, half * 128 : half * 128 + 128] = jnp.concatenate(
                [top, motion - top, one, two, three, jnp.zeros((8, 128), jnp.float32)], axis=0
            ).astype(jnp.bfloat16)
        return carry

    lax.fori_loop(0, BLOCKS // 2, split, 0)

    slot = lax.broadcasted_iota(jnp.int32, (PLACED, 256), 0).astype(jnp.float32)

    def place_chunk(s, carry):
        begin = (s * PLACED).astype(jnp.float32)
        total = jnp.zeros((80, PLACED), jnp.float32)
        for i in range(BLOCKS // 2):
            hit = (slot == (order[i : i + 1, :] - begin)).astype(jnp.float32).astype(jnp.bfloat16)
            total = total + whole_dot(parts[i], hit, (((1,), (1,)), ((), ())))
        short = total[0:48].astype(jnp.bfloat16)
        weights[2 * s] = short[:, 0:128]
        weights[2 * s + 1] = short[:, 128:256]
        spot = (total[48:56] + total[56:64]) + total[64:72]
        for half in range(2):
            piece = jnp.concatenate(
                [spot[:, half * 128 : half * 128 + 128], jnp.zeros((120, 128), jnp.float32)], axis=0
            ).T
            at = pl.multiple_of(s * PLACED + half * 128, 128)
            for c in range(3):
                centres[c, pl.ds(at, 128), :] = jnp.broadcast_to(piece[:, c : c + 1], (128, 128))
        return carry

    lax.fori_loop(0, (found + (PLACED - 1)) // PLACED, place_chunk, 0)

    for j in range(8):

        def add(chunk, sums, j=j):
            at = pl.multiple_of(chunk * CHUNK, CHUNK)
            spot = [centres[c, pl.ds(at, CHUNK), :] for c in range(3)]
            pieces = weights[chunk]
            result = []
            for p in range(2):
                tops, rests = [], []
                for half in range(2):
                    square = None
                    for c in range(3):
                        gap = spot[c] - nodes[c, p, j : j + 1, half * 128 : half * 128 + 128]
                        square = gap * gap if square is None else square + gap * gap
                    radius = square * lax.rsqrt(jnp.maximum(square, 1e-30))
                    rest = jnp.maximum(1.0 - radius, 0.0)
                    rest = rest * rest
                    value = rest * rest * (4.0 * radius + 1.0)
                    top = value.astype(jnp.bfloat16)
                    tops.append(top)
                    rests.append((value - top.astype(jnp.float32)).astype(jnp.bfloat16))
                full = whole_dot(pieces, jnp.concatenate(tops, axis=1))
                extra = whole_dot(pieces[0:32], jnp.concatenate(rests, axis=1))
                result.append(sums[p] + (full[0:24] + (full[24:48] + extra[0:24])))
            return tuple(result)

        zero = jnp.zeros((24, 256), jnp.float32)
        sums = lax.fori_loop(ends[0, j], ends[1, j], add, (zero, zero))
        for p in range(2):
            for c in range(3):
                value = sums[p][c * 8 : c * 8 + 8]
                moved_ref[:, c, p, j, :] = value
                deformed_ref[:, c, p, j, :] = value + base[2 * c + p][j : j + 1]


def evaluate(gathered, base_nodes, place):
    shape = jax.ShapeDtypeStruct((INST, 3, 2, 8, 256), jnp.float32)
    return pl.pallas_call(
        lambda *refs: evaluate_kernel(place, *refs),
        out_shape=(shape, shape),
        in_specs=[vmem()] * 2,
        out_specs=(vmem(), vmem()),
        scratch_shapes=[
            pltpu.VMEM((3, 2, 8, 256), jnp.float32),
            pltpu.VMEM((BLOCKS // 2, 80, 256), jnp.bfloat16),
            pltpu.VMEM((BLOCKS // 2, 256), jnp.float32),
            pltpu.VMEM((NC // CHUNK, 48, CHUNK), jnp.bfloat16),
            pltpu.VMEM((3, NC, 128), jnp.float32),
            pltpu.SMEM((2, 8), jnp.int32),
        ],
        compiler_params=params(),
        name="evaluate",
    )(gathered, base_nodes)


def shifted(value, axis):
    extent = value.shape[axis]
    at = lax.broadcasted_iota(jnp.int32, value.shape, axis)
    following = pltpu.roll(value, extent - 1, axis)
    preceding = pltpu.roll(value, 1, axis)
    upper = jnp.where(at == extent - 1, 2.0 * value - preceding, following)
    lower = jnp.where(at == 0, 2.0 * value - following, preceding)
    return (upper - lower) * 0.5


def cross(a, b):
    return [
        a[1] * b[2] - a[2] * b[1],
        a[2] * b[0] - a[0] * b[2],
        a[0] * b[1] - a[1] * b[0],
    ]


def exchange_kernel(moved_ref, deformed_ref, n_ref, disp_ref, metrics_ref, halo, send, recv, local):
    inst, space = lax.axis_index("inst"), lax.axis_index("space")
    behind, ahead = lax.rem(space + SPACE - 1, SPACE), lax.rem(space + 1, SPACE)
    barrier = pltpu.get_barrier_semaphore()
    targets = [lax.rem(inst + k, INST) for k in range(INST)]
    peers = [(t, s) for t in targets for s in (behind, ahead)] + [(t, space) for t in targets[1:]]
    for peer in peers:
        pl.semaphore_signal(barrier, inc=1, device_id=peer, device_id_type=MESH)
    pl.semaphore_wait(barrier, len(peers))
    rows = pl.ds(pl.multiple_of(inst * 8, 8), 8)
    copies = []

    def start(source, target, kind, k, device):
        copy = pltpu.make_async_remote_copy(
            src_ref=source,
            dst_ref=target,
            send_sem=send.at[kind, k],
            recv_sem=recv.at[kind, k],
            device_id=device,
            device_id_type=MESH,
        )
        copy.start()
        copies.append(copy)

    for k, t in enumerate(targets):
        start(deformed_ref.at[t, :, 0], halo.at[1, :, rows, :], 0, k, (t, behind))
        start(deformed_ref.at[t, :, 1], halo.at[0, :, rows, :], 1, k, (t, ahead))
        if k:
            start(moved_ref.at[t], disp_ref.at[0, :, :, rows, :], 2, k, (t, space))
    mine = pltpu.make_async_copy(moved_ref.at[inst], disp_ref.at[0, :, :, rows, :], local)
    mine.start()
    mine.wait()
    for copy in copies:
        copy.wait()
    for p in range(2):
        here = [n_ref[c, p] + disp_ref[0, c, p] for c in range(3)]
        there = [n_ref[c, 1 - p] + disp_ref[0, c, 1 - p] for c in range(3)]
        along_i = []
        for c in range(3):
            if p == 0:
                beyond = jnp.where(space == 0, 2.0 * here[c] - there[c], halo[0, c])
                along_i.append((there[c] - beyond) * 0.5)
            else:
                beyond = jnp.where(space == SPACE - 1, 2.0 * here[c] - there[c], halo[1, c])
                along_i.append((beyond - there[c]) * 0.5)
        along_j = [shifted(value, 0) for value in here]
        along_k = [shifted(value, 1) for value in here]
        one = cross(along_j, along_k)
        for c in range(3):
            metrics_ref[0, c, p] = one[c]
        metrics_ref[0, 9, p] = along_i[0] * one[0] + along_i[1] * one[1] + along_i[2] * one[2]
        two = cross(along_k, along_i)
        for c in range(3):
            metrics_ref[0, 3 + c, p] = two[c]
        three = cross(along_i, along_j)
        for c in range(3):
            metrics_ref[0, 6 + c, p] = three[c]


def exchange(moved, deformed, base_nodes):
    return pl.pallas_call(
        exchange_kernel,
        out_shape=(
            jax.ShapeDtypeStruct((1,) + base_nodes.shape, jnp.float32),
            jax.ShapeDtypeStruct((1, 10) + base_nodes.shape[1:], jnp.float32),
        ),
        in_specs=[vmem()] * 3,
        out_specs=(vmem(), vmem()),
        scratch_shapes=[
            pltpu.VMEM((2, 3) + base_nodes.shape[2:], jnp.float32),
            pltpu.SemaphoreType.DMA((3, INST)),
            pltpu.SemaphoreType.DMA((3, INST)),
            pltpu.SemaphoreType.DMA,
        ],
        compiler_params=params(collective_id=1, has_side_effects=True),
        name="exchange",
    )(moved, deformed, base_nodes)


def body(amplitudes, modal_coeffs, centre_positions, base_nodes):
    gathered = gather(amplitudes, modal_coeffs, centre_positions)
    moved, deformed = evaluate(gathered, base_nodes, lambda: lax.axis_index("inst"))
    return exchange(moved, deformed, base_nodes)


def solution(mesh):
    in_specs = (
        P(),
        P(None, None, ("inst", "space")),
        P(None, ("inst", "space")),
        P(None, "space", None, None),
    )
    out_specs = (P("inst", None, "space", None, None), P("inst", None, "space", None, None))
    return jax.shard_map(body, mesh=mesh, in_specs=in_specs, out_specs=out_specs, check_vma=False)
```

```python
import jax
import jax.numpy as jnp
from jax import lax
from jax.experimental import pallas as pl
from jax.experimental.pallas import tpu as pltpu
from jax.sharding import PartitionSpec as P

MESH = pl.DeviceIdType.MESH
HIGH = lax.Precision.HIGHEST
XS, YS, ZS, CORES = 4, 4, 16, 2
INST, SPACE = YS * CORES, XS * ZS
OWN = 8
BLOCKS = XS * YS * CORES
NC = BLOCKS * ZS * OWN
VALUES = 32
BINS = 32
CHUNK = 128
PLACED = 256
MARGIN = 1.0 + 2.0**-11
VMEM_LIMIT = 48 * 1024 * 1024


def vmem():
    return pl.BlockSpec(memory_space=pltpu.VMEM)


def params(**more):
    return pltpu.CompilerParams(vmem_limit_bytes=VMEM_LIMIT, **more)


def swap_blocks(arrays):
    block = lax.broadcasted_iota(jnp.int32, arrays[0].shape, 1) // 16
    arrays = list(arrays)
    for step in (1, 2, 4):
        upper = (block & step) != 0
        for a in range(8):
            if not a & step:
                one, two = arrays[a], arrays[a | step]
                arrays[a] = jnp.where(upper, pltpu.roll(two, 16 * step, 1), one)
                arrays[a | step] = jnp.where(upper, two, pltpu.roll(one, 128 - 16 * step, 1))
    return arrays


def gather_kernel(own_ref, strip, out_ref, tiles, zbuf, send, recv):
    inst, space = lax.axis_index("inst"), lax.axis_index("space")
    y, core = inst // CORES, inst % CORES
    x, z = space // ZS, space % ZS
    z_peers = [(inst, x * ZS + lax.rem(z + k, ZS)) for k in range(1, ZS)]
    steps = [(a, b) for a in range(YS) for b in range(XS) if a or b]
    plane_peers = [
        (lax.rem(y + a, YS) * CORES + core, lax.rem(x + b, XS) * ZS + z) for a, b in steps
    ]
    other = (y * CORES + (1 - core), space)
    peers = z_peers + plane_peers + [other]
    barrier = pltpu.get_barrier_semaphore()
    for peer in peers:
        pl.semaphore_signal(barrier, inc=1, device_id=peer, device_id_type=MESH)

    transposed = (((1,), (1,)), ((), ()))

    def high_dot(a, b):
        return lax.dot_general(a, b, transposed, precision=HIGH, preferred_element_type=jnp.float32)

    amp = own_ref[24:32]
    eye = (
        lax.broadcasted_iota(jnp.int32, (OWN, OWN), 0) == lax.broadcasted_iota(jnp.int32, (OWN, OWN), 1)
    ).astype(jnp.float32)
    own = [high_dot(own_ref[8 * c : 8 * c + 8], amp) for c in range(3)]
    own.append(high_dot(eye, own_ref[32:40, 0:OWN])[:, 0:3])
    own = jnp.concatenate(own + [jnp.zeros((OWN, 128 - 27), jnp.float32)], axis=1)
    row_id = lax.broadcasted_iota(jnp.int32, (OWN, 128), 0) % 4
    spread = jnp.zeros((OWN, 128), jnp.float32)
    for a in range(4):
        moved = own if a == 0 else pltpu.roll(own, VALUES * a, 1)
        spread = spread + jnp.where(row_id == a, moved, 0.0)
    zbuf[z] = jnp.concatenate(
        [
            jnp.sum(spread[0:4], axis=0, keepdims=True),
            jnp.sum(spread[4:8], axis=0, keepdims=True),
        ],
        axis=0,
    )

    for half in range(2):
        lanes = slice(half * 128, half * 128 + 128)
        rows = [
            jnp.concatenate(
                [strip[c, p, j : j + 1, lanes] for c in range(3) for p in range(2)]
                + [jnp.zeros((2, 128), jnp.float32)],
                axis=0,
            )
            for j in range(8)
        ]
        for t, tile in enumerate(swap_blocks(rows)):
            tiles[8 * half + t] = tile * 0.25
    pl.semaphore_wait(barrier, len(peers))

    def start(ref, k, peer):
        copy = pltpu.make_async_remote_copy(
            src_ref=ref,
            dst_ref=ref,
            send_sem=send.at[k],
            recv_sem=recv.at[k],
            device_id=peer,
            device_id_type=MESH,
        )
        copy.start()
        return copy

    far_first = sorted(range(ZS - 1), key=lambda k: -min(k + 1, ZS - 1 - k))
    copies = [start(zbuf.at[z], k, z_peers[k]) for k in far_first]
    for copy in reversed(copies):
        copy.wait()
    rows = jnp.concatenate([zbuf[i] for i in range(ZS)], axis=0)
    rows = jnp.concatenate([rows, jnp.zeros((128 - 2 * ZS, 128), jnp.float32)], axis=0).T
    block = rows[0:VALUES]
    for a in range(1, 4):
        block = block + pltpu.roll(rows[VALUES * a : VALUES * (a + 1)], VALUES * a, 1)
    mine = core * (XS * YS) + y * XS + x
    out_ref[mine] = block

    def hops(k):
        a, b = steps[k]
        return min(a, YS - a) + min(b, XS - b)

    far_first = sorted(range(len(steps)), key=lambda k: -hops(k))
    copies = [start(out_ref.at[mine], ZS - 1 + k, plane_peers[k]) for k in far_first]
    passed = [start(out_ref.at[mine], ZS - 1 + len(steps), other)]
    for copy, k in reversed(list(zip(copies, far_first))):
        copy.wait_recv()
        a, b = steps[k]
        origin = core * (XS * YS) + lax.rem(y + YS - a, YS) * XS + lax.rem(x + XS - b, XS)
        passed.append(start(out_ref.at[origin], ZS + len(steps) + k, other))
    for copy in copies:
        copy.wait_send()
    for copy in passed:
        copy.wait()


def gather(own, strip):
    count = ZS + 2 * XS * YS - 2
    return pl.pallas_call(
        gather_kernel,
        out_shape=(
            jax.ShapeDtypeStruct((BLOCKS, VALUES, 128), jnp.float32),
            jax.ShapeDtypeStruct((16, 8, 128), jnp.float32),
        ),
        in_specs=[vmem()] * 2,
        out_specs=(vmem(), vmem()),
        scratch_shapes=[
            pltpu.VMEM((ZS, 2, 128), jnp.float32),
            pltpu.SemaphoreType.DMA((count,)),
            pltpu.SemaphoreType.DMA((count,)),
        ],
        compiler_params=params(collective_id=0, has_side_effects=True),
        name="gather",
    )(own, strip)


def whole_dot(a, b, precision=None):
    return jnp.dot(a, b, precision=precision, preferred_element_type=jnp.float32)


def evaluate_kernel(g_ref, strip, tiles, moved_ref, deformed_ref, nodes, parts, order, weights, centres, found, edges, ends, arrived):
    nodes[...] = strip[...] * 0.25

    spots = [g_ref[:, 24 + c, :] * 0.25 for c in range(3)]
    near = None
    for c in range(3):
        low = jnp.min(nodes[c]) - MARGIN
        high = jnp.max(nodes[c]) + MARGIN
        inside = (spots[c] >= low) & (spots[c] <= high)
        near = inside if near is None else near & inside
        if c == 2:
            k_low, scale = low, BINS / jnp.full((1, 1), high - low)

    def bin_of(value):
        return jnp.clip(jnp.floor((value - k_low) * scale), 0.0, BINS - 1.0)

    bins = jnp.where(near, bin_of(spots[2]), -1.0)

    bin_id = lax.broadcasted_iota(jnp.int32, (BINS, 128), 0).astype(jnp.float32)
    member = jnp.concatenate(
        [(bins[i : i + 1] == bin_id).astype(jnp.float32) for i in range(BLOCKS)], axis=0
    )
    lane = lax.broadcasted_iota(jnp.int32, (128, 256), 1)
    counting = ((lax.broadcasted_iota(jnp.int32, (128, 256), 0) <= lane) | (lane >= 128)).astype(jnp.float32)
    counts = whole_dot(member.astype(jnp.bfloat16), counting.astype(jnp.bfloat16))
    total = counts[0:BINS, 128:256]
    for i in range(1, BLOCKS):
        total = total + counts[i * BINS : (i + 1) * BINS, 128:256]
    earlier = (
        lax.broadcasted_iota(jnp.int32, (BINS, BINS), 1) < lax.broadcasted_iota(jnp.int32, (BINS, BINS), 0)
    ).astype(jnp.float32)
    running = whole_dot(earlier, total, HIGH)
    rows = []
    for i in range(BLOCKS):
        own = slice(i * BINS, (i + 1) * BINS)
        rows.append(jnp.sum(member[own] * (running + counts[own, 0:128]), axis=0, keepdims=True) - 1.0)
        running = running + counts[own, 128:256]
    position = jnp.concatenate(rows + [jnp.zeros((128 - BLOCKS, 128), jnp.float32)], axis=0).T
    for i in range(BLOCKS):
        order[i * 128 : i * 128 + 128, :] = jnp.broadcast_to(position[:, i : i + 1], (128, 128))

    k_min = jnp.min(jnp.min(nodes[2], axis=0), axis=0, keepdims=True)
    k_max = jnp.max(jnp.max(nodes[2], axis=0), axis=0, keepdims=True)
    for step in (1, 2, 4, 8):
        k_min = jnp.minimum(k_min, pltpu.roll(k_min, step, 1))
        k_max = jnp.maximum(k_max, pltpu.roll(k_max, step, 1))
    wide_id = lax.broadcasted_iota(jnp.int32, (BINS, 256), 0).astype(jnp.float32)
    wide_total = jnp.concatenate([total, total], axis=1)
    start = jnp.sum(jnp.where(wide_id < bin_of(k_min - MARGIN), wide_total, 0.0), axis=0, keepdims=True)
    stop = jnp.sum(jnp.where(wide_id <= bin_of(k_max + MARGIN), wide_total, 0.0), axis=0, keepdims=True)
    edges[0:1, :] = jnp.floor(start * (1.0 / CHUNK)).astype(jnp.int32)
    edges[1:2, :] = jnp.floor((stop + (CHUNK - 1.0)) * (1.0 / CHUNK)).astype(jnp.int32)
    edges[2:3, :] = jnp.floor(
        (jnp.sum(wide_total, axis=0, keepdims=True) + (PLACED - 1.0)) * (1.0 / PLACED)
    ).astype(jnp.int32)
    copy = pltpu.make_async_copy(edges, ends, arrived)
    copy.start()

    def split(i, carry):
        for half in range(2):
            value = g_ref[2 * i + half]
            motion = value[0:24]
            top = motion.astype(jnp.bfloat16).astype(jnp.float32)
            spot = value[24:32] * 0.25
            one = spot.astype(jnp.bfloat16).astype(jnp.float32)
            two = (spot - one).astype(jnp.bfloat16).astype(jnp.float32)
            three = spot - one - two
            parts[i, :, half * 128 : half * 128 + 128] = jnp.concatenate(
                [top, motion - top, one, two, three, jnp.zeros((8, 128), jnp.float32)], axis=0
            ).astype(jnp.bfloat16)
        return carry

    lax.fori_loop(0, BLOCKS // 2, split, 0)
    copy.wait()

    slot = lax.broadcasted_iota(jnp.int32, (1, 128), 1)

    def place_chunk(s, carry):
        sums = jnp.zeros((80, PLACED), jnp.float32)
        wanted = [(slot + (s * PLACED + 128 * half)).astype(jnp.float32) for half in range(2)]
        for i in range(BLOCKS // 2):
            at = order[i * 256 : i * 256 + 256, :]
            hit = jnp.concatenate([(at == w).astype(jnp.float32) for w in wanted], axis=1)
            sums = sums + whole_dot(parts[i], hit.astype(jnp.bfloat16))
        short = sums[0:48].astype(jnp.bfloat16)
        spot = (sums[48:56] + sums[56:64]) + sums[64:72]
        for half in range(2):
            lanes = slice(half * 128, half * 128 + 128)
            weights[2 * s + half] = short[:, lanes]
            piece = jnp.concatenate([spot[:, lanes], jnp.zeros((120, 128), jnp.float32)], axis=0).T
            at = pl.multiple_of(s * PLACED + half * 128, 128)
            for c in range(3):
                centres[c, pl.ds(at, 128), :] = jnp.broadcast_to(piece[:, c : c + 1], (128, 128))
        return carry

    lax.fori_loop(0, ends[2, 0], place_chunk, 0)

    for t in range(16):

        def add(chunk, sums, t=t):
            at = pl.multiple_of(chunk * CHUNK, CHUNK)
            spot = [centres[c, pl.ds(at, CHUNK), :] for c in range(3)]
            pieces = weights[chunk]
            tops, rests = [], []
            for p in range(2):
                square = None
                for c in range(3):
                    gap = spot[c] - tiles[t, 2 * c + p : 2 * c + p + 1, :]
                    square = gap * gap if square is None else square + gap * gap
                radius = square * lax.rsqrt(jnp.maximum(square, 1e-30))
                rest = jnp.maximum(1.0 - radius, 0.0)
                rest = rest * rest
                value = rest * rest * (4.0 * radius + 1.0)
                top = value.astype(jnp.bfloat16)
                tops.append(top)
                rests.append((value - top.astype(jnp.float32)).astype(jnp.bfloat16))
            full = whole_dot(pieces, jnp.concatenate(tops, axis=1))
            extra = whole_dot(pieces[0:32], jnp.concatenate(rests, axis=1))
            return sums + (full[0:24] + (full[24:48] + extra[0:24]))

        last = 16 * t + 15
        found[t] = lax.fori_loop(ends[0, last], ends[1, last], add, jnp.zeros((24, 256), jnp.float32))

    for p in range(2):
        for half in range(2):
            lanes = slice(half * 128, half * 128 + 128)
            rows = swap_blocks([found[8 * half + t, :, p * 128 : p * 128 + 128] for t in range(8)])
            for j in range(8):
                for c in range(3):
                    value = rows[j][c * 8 : c * 8 + 8]
                    into = pl.ds(c * 32 + p * 16 + half * 8 + j, 8, stride=96)
                    moved_ref[into, :] = value
                    deformed_ref[into, :] = value + strip[c, p, j : j + 1, lanes]


def evaluate(gathered, strip, tiles):
    shape = jax.ShapeDtypeStruct((INST * 96, 128), jnp.float32)
    results = pl.pallas_call(
        evaluate_kernel,
        out_shape=(shape, shape),
        in_specs=[vmem()] * 3,
        out_specs=(vmem(), vmem()),
        scratch_shapes=[
            pltpu.VMEM((3, 2, 8, 256), jnp.float32),
            pltpu.VMEM((BLOCKS // 2, 80, 256), jnp.bfloat16),
            pltpu.VMEM((NC, 128), jnp.float32),
            pltpu.VMEM((NC // CHUNK, 48, CHUNK), jnp.bfloat16),
            pltpu.VMEM((3, NC, 128), jnp.float32),
            pltpu.VMEM((16, 24, 256), jnp.float32),
            pltpu.VMEM((8, 256), jnp.int32),
            pltpu.SMEM((8, 256), jnp.int32),
            pltpu.SemaphoreType.DMA,
        ],
        compiler_params=params(),
        name="evaluate",
    )(gathered, strip, tiles)
    return [value.reshape(INST, 3, 2, 2, 8, 128) for value in results]


def exchange_kernel(moved_ref, deformed_ref, own, halo, send, recv, local):
    inst, space = lax.axis_index("inst"), lax.axis_index("space")
    behind, ahead = lax.rem(space + SPACE - 1, SPACE), lax.rem(space + 1, SPACE)
    barrier = pltpu.get_barrier_semaphore()
    targets = [lax.rem(inst + k, INST) for k in range(INST)]
    peers = [(t, s) for t in targets for s in (behind, ahead)] + [(t, space) for t in targets[1:]]
    for peer in peers:
        pl.semaphore_signal(barrier, inc=1, device_id=peer, device_id_type=MESH)
    rows = pl.ds(pl.multiple_of(inst * 8, 8), 8)
    stays = pltpu.make_async_copy(moved_ref.at[inst], own.at[:, :, :, rows, :], local)
    stays.start()
    pl.semaphore_wait(barrier, len(peers))
    copies = []

    def start(source, target, kind, k, device):
        copy = pltpu.make_async_remote_copy(
            src_ref=source,
            dst_ref=target,
            send_sem=send.at[kind, k],
            recv_sem=recv.at[kind, k],
            device_id=device,
            device_id_type=MESH,
        )
        copy.start()
        copies.append(copy)

    for k in (4, 3, 5, 2, 6, 1, 7, 0):
        t = targets[k]
        start(deformed_ref.at[t, :, 0], halo.at[1, :, :, rows, :], 0, k, (t, behind))
        start(deformed_ref.at[t, :, 1], halo.at[0, :, :, rows, :], 1, k, (t, ahead))
        if k:
            start(moved_ref.at[t], own.at[:, :, :, rows, :], 2, k, (t, space))
    for copy in [stays] + copies:
        copy.wait()


def exchange(moved, deformed, rows, width):
    return pl.pallas_call(
        exchange_kernel,
        out_shape=(
            jax.ShapeDtypeStruct((3, 2, 2, rows, width), jnp.float32),
            jax.ShapeDtypeStruct((2, 3, 2, rows, width), jnp.float32),
        ),
        in_specs=[vmem(), vmem()],
        out_specs=(vmem(), vmem()),
        scratch_shapes=[
            pltpu.SemaphoreType.DMA((3, INST)),
            pltpu.SemaphoreType.DMA((3, INST)),
            pltpu.SemaphoreType.DMA,
        ],
        compiler_params=params(collective_id=1, has_side_effects=True),
        name="exchange",
    )(moved, deformed)


def shifted(value, axis):
    extent = value.shape[axis]
    at = lax.broadcasted_iota(jnp.int32, value.shape, axis)
    following = pltpu.roll(value, extent - 1, axis)
    preceding = pltpu.roll(value, 1, axis)
    upper = jnp.where(at == extent - 1, 2.0 * value - preceding, following)
    lower = jnp.where(at == 0, 2.0 * value - following, preceding)
    return (upper - lower) * 0.5


def cross(a, b):
    return [
        a[1] * b[2] - a[2] * b[1],
        a[2] * b[0] - a[0] * b[2],
        a[0] * b[1] - a[1] * b[0],
    ]


def metrics_kernel(own, halo, n_ref, disp_hbm, metrics_hbm, disp, metrics, sems):
    space = lax.axis_index("space")
    copies = []

    def leave(source, target):
        copy = pltpu.make_async_copy(source, target, sems.at[len(copies)])
        copy.start()
        copies.append(copy)

    for c in range(3):
        for p in range(2):
            for half in range(2):
                disp[c, p, :, half * 128 : half * 128 + 128] = own[c, p, half]
    leave(disp, disp_hbm.at[0])

    def beside(which, c):
        return jnp.concatenate([halo[which, c, 0], halo[which, c, 1]], axis=1)

    for p in range(2):
        here = [n_ref[c, p] + disp[c, p] for c in range(3)]
        there = [n_ref[c, 1 - p] + disp[c, 1 - p] for c in range(3)]
        along_i = []
        for c in range(3):
            if p == 0:
                beyond = jnp.where(space == 0, 2.0 * here[c] - there[c], beside(0, c))
                along_i.append((there[c] - beyond) * 0.5)
            else:
                beyond = jnp.where(space == SPACE - 1, 2.0 * here[c] - there[c], beside(1, c))
                along_i.append((beyond - there[c]) * 0.5)
        along_j = [shifted(value, 0) for value in here]
        along_k = [shifted(value, 1) for value in here]
        one = cross(along_j, along_k)
        two = cross(along_k, along_i)
        three = cross(along_i, along_j)
        last = along_i[0] * one[0] + along_i[1] * one[1] + along_i[2] * one[2]
        for row, value in enumerate(one + two + three + [last]):
            metrics[p, row] = value
        leave(metrics.at[p], metrics_hbm.at[0, :, p])
    for copy in copies:
        copy.wait()


def metric_rows(own, halo, base_nodes):
    anywhere = pl.BlockSpec(memory_space=pltpu.HBM)
    return pl.pallas_call(
        metrics_kernel,
        out_shape=(
            jax.ShapeDtypeStruct((1,) + base_nodes.shape, jnp.float32),
            jax.ShapeDtypeStruct((1, 10) + base_nodes.shape[1:], jnp.float32),
        ),
        in_specs=[vmem()] * 3,
        out_specs=(anywhere, anywhere),
        scratch_shapes=[
            pltpu.VMEM(base_nodes.shape, jnp.float32),
            pltpu.VMEM((2, 10) + base_nodes.shape[2:], jnp.float32),
            pltpu.SemaphoreType.DMA((3,)),
        ],
        compiler_params=params(),
        name="metrics",
    )(own, halo, base_nodes)


def body(amplitudes, modal_coeffs, centre_positions, base_nodes):
    modes = amplitudes.shape[1]
    own = jnp.concatenate(
        [
            modal_coeffs.transpose(1, 2, 0).reshape(3 * OWN, modes),
            amplitudes,
            jnp.pad(centre_positions, ((0, 5), (0, modes - OWN))),
        ],
        axis=0,
    )
    strip = lax.dynamic_slice_in_dim(base_nodes, lax.axis_index("inst") * 8, 8, 2)
    gathered, tiles = gather(own, strip)
    moved, deformed = evaluate(gathered, strip, tiles)
    rows, width = base_nodes.shape[2], base_nodes.shape[3] // 2
    own, halo = exchange(moved, deformed, rows, width)
    return metric_rows(own, halo, base_nodes)


def solution(mesh):
    in_specs = (
        P(),
        P(None, None, ("inst", "space")),
        P(None, ("inst", "space")),
        P(None, "space", None, None),
    )
    out_specs = (P("inst", None, "space", None, None), P("inst", None, "space", None, None))
    return jax.shard_map(body, mesh=mesh, in_specs=in_specs, out_specs=out_specs, check_vma=False)
```

```python
import jax
import jax.numpy as jnp
from jax import lax
from jax.experimental import pallas as pl
from jax.experimental.pallas import tpu as pltpu
from jax.sharding import PartitionSpec as P

MESH = pl.DeviceIdType.MESH
HIGH = lax.Precision.HIGHEST
XS, YS, ZS, CORES = 4, 4, 16, 2
INST, SPACE = YS * CORES, XS * ZS
OWN = 8
BLOCKS = XS * YS * CORES
NC = BLOCKS * ZS * OWN
VALUES = 32
BINS = 32
CHUNK = 128
GROUP = 8
PLACED = 256
MARGIN = 1.0 + 2.0**-11
VMEM_LIMIT = 48 * 1024 * 1024


def vmem():
    return pl.BlockSpec(memory_space=pltpu.VMEM)


def params(**more):
    return pltpu.CompilerParams(vmem_limit_bytes=VMEM_LIMIT, **more)


def swap_blocks(arrays):
    block = lax.broadcasted_iota(jnp.int32, arrays[0].shape, 1) // 16
    arrays = list(arrays)
    for step in (1, 2, 4):
        upper = (block & step) != 0
        for a in range(8):
            if not a & step:
                one, two = arrays[a], arrays[a | step]
                arrays[a] = jnp.where(upper, pltpu.roll(two, 16 * step, 1), one)
                arrays[a | step] = jnp.where(upper, two, pltpu.roll(one, 128 - 16 * step, 1))
    return arrays


def gather_kernel(own_ref, out_ref, zbuf, send, recv):
    inst, space = lax.axis_index("inst"), lax.axis_index("space")
    y, core = inst // CORES, inst % CORES
    x, z = space // ZS, space % ZS
    z_peers = [(inst, x * ZS + lax.rem(z + k, ZS)) for k in range(1, ZS)]
    steps = [(a, b) for a in range(YS) for b in range(XS) if a or b]
    plane_peers = [
        (lax.rem(y + a, YS) * CORES + core, lax.rem(x + b, XS) * ZS + z) for a, b in steps
    ]
    other = (y * CORES + (1 - core), space)
    peers = z_peers + plane_peers + [other]
    barrier = pltpu.get_barrier_semaphore()
    for peer in peers:
        pl.semaphore_signal(barrier, inc=1, device_id=peer, device_id_type=MESH)

    transposed = (((1,), (1,)), ((), ()))

    def high_dot(a, b):
        return lax.dot_general(a, b, transposed, precision=HIGH, preferred_element_type=jnp.float32)

    amp = own_ref[24:32]
    eye = (
        lax.broadcasted_iota(jnp.int32, (OWN, OWN), 0) == lax.broadcasted_iota(jnp.int32, (OWN, OWN), 1)
    ).astype(jnp.float32)
    own = [high_dot(own_ref[8 * c : 8 * c + 8], amp) for c in range(3)]
    own.append(high_dot(eye, own_ref[32:40, 0:OWN])[:, 0:3])
    own = jnp.concatenate(own + [jnp.zeros((OWN, 128 - 27), jnp.float32)], axis=1)
    row_id = lax.broadcasted_iota(jnp.int32, (OWN, 128), 0) % 4
    spread = jnp.zeros((OWN, 128), jnp.float32)
    for a in range(4):
        moved = own if a == 0 else pltpu.roll(own, VALUES * a, 1)
        spread = spread + jnp.where(row_id == a, moved, 0.0)
    zbuf[z] = jnp.concatenate(
        [
            jnp.sum(spread[0:4], axis=0, keepdims=True),
            jnp.sum(spread[4:8], axis=0, keepdims=True),
        ],
        axis=0,
    )

    pl.semaphore_wait(barrier, len(peers))

    def start(ref, k, peer):
        copy = pltpu.make_async_remote_copy(
            src_ref=ref,
            dst_ref=ref,
            send_sem=send.at[k],
            recv_sem=recv.at[k],
            device_id=peer,
            device_id_type=MESH,
        )
        copy.start()
        return copy

    far_first = sorted(range(ZS - 1), key=lambda k: -min(k + 1, ZS - 1 - k))
    copies = [start(zbuf.at[z], k, z_peers[k]) for k in far_first]
    for copy in reversed(copies):
        copy.wait()
    rows = jnp.concatenate([zbuf[i] for i in range(ZS)], axis=0)
    rows = jnp.concatenate([rows, jnp.zeros((128 - 2 * ZS, 128), jnp.float32)], axis=0).T
    block = rows[0:VALUES]
    for a in range(1, 4):
        block = block + pltpu.roll(rows[VALUES * a : VALUES * (a + 1)], VALUES * a, 1)
    mine = core * (XS * YS) + y * XS + x
    out_ref[mine] = block

    def hops(k):
        a, b = steps[k]
        return min(a, YS - a) + min(b, XS - b)

    far_first = sorted(range(len(steps)), key=lambda k: -hops(k))
    copies = [start(out_ref.at[mine], ZS - 1 + k, plane_peers[k]) for k in far_first]
    passed = [start(out_ref.at[mine], ZS - 1 + len(steps), other)]
    for copy, k in reversed(list(zip(copies, far_first))):
        copy.wait_recv()
        a, b = steps[k]
        origin = core * (XS * YS) + lax.rem(y + YS - a, YS) * XS + lax.rem(x + XS - b, XS)
        passed.append(start(out_ref.at[origin], ZS + len(steps) + k, other))
    for copy in copies:
        copy.wait_send()
    for copy in passed:
        copy.wait()


def gather(own):
    count = ZS + 2 * XS * YS - 2
    return pl.pallas_call(
        gather_kernel,
        out_shape=jax.ShapeDtypeStruct((BLOCKS, VALUES, 128), jnp.float32),
        in_specs=[vmem()],
        out_specs=vmem(),
        scratch_shapes=[
            pltpu.VMEM((ZS, 2, 128), jnp.float32),
            pltpu.SemaphoreType.DMA((count,)),
            pltpu.SemaphoreType.DMA((count,)),
        ],
        compiler_params=params(collective_id=0, has_side_effects=True),
        cost_estimate=pl.CostEstimate(flops=10**9, bytes_accessed=2 * 10**7, transcendentals=0),
        name="gather",
    )(own)


def whole_dot(a, b, precision=None):
    return jnp.dot(a, b, precision=precision, preferred_element_type=jnp.float32)


def evaluate_kernel(g_ref, n_ref, moved_ref, deformed_ref, kept, strip, tiles, nodes, parts, order, weights, windows, centres, found, edges, ends, arrived, passing):
    keep = pltpu.make_async_copy(n_ref, kept, passing)
    keep.start()
    first = pl.multiple_of(lax.axis_index("inst") * 8, 8)
    strip[...] = n_ref[:, :, pl.ds(first, 8), :]
    nodes[...] = strip[...] * 0.25

    for half in range(2):
        lanes = slice(half * 128, half * 128 + 128)
        rows = [
            jnp.concatenate(
                [strip[c, p, j : j + 1, lanes] for c in range(3) for p in range(2)]
                + [jnp.zeros((2, 128), jnp.float32)],
                axis=0,
            )
            for j in range(8)
        ]
        for t, tile in enumerate(swap_blocks(rows)):
            tiles[8 * half + t] = tile * 0.25
    spots = [g_ref[:, 24 + c, :] * 0.25 for c in range(3)]
    near = None
    for c in range(3):
        low = jnp.min(nodes[c]) - MARGIN
        high = jnp.max(nodes[c]) + MARGIN
        inside = (spots[c] >= low) & (spots[c] <= high)
        near = inside if near is None else near & inside
        if c == 2:
            k_low, scale = low, BINS / jnp.full((1, 1), high - low)

    def bin_of(value):
        return jnp.clip(jnp.floor((value - k_low) * scale), 0.0, BINS - 1.0)

    bins = jnp.where(near, bin_of(spots[2]), -1.0)

    bin_id = lax.broadcasted_iota(jnp.int32, (BINS, 128), 0).astype(jnp.float32)
    member = jnp.concatenate(
        [(bins[i : i + 1] == bin_id).astype(jnp.float32) for i in range(BLOCKS)], axis=0
    )
    lane = lax.broadcasted_iota(jnp.int32, (128, 256), 1)
    counting = ((lax.broadcasted_iota(jnp.int32, (128, 256), 0) <= lane) | (lane >= 128)).astype(jnp.float32)
    counts = whole_dot(member.astype(jnp.bfloat16), counting.astype(jnp.bfloat16))
    total = counts[0:BINS, 128:256]
    for i in range(1, BLOCKS):
        total = total + counts[i * BINS : (i + 1) * BINS, 128:256]
    earlier = (
        lax.broadcasted_iota(jnp.int32, (BINS, BINS), 1) < lax.broadcasted_iota(jnp.int32, (BINS, BINS), 0)
    ).astype(jnp.float32)
    running = whole_dot(earlier, total, HIGH)
    rows = []
    for i in range(BLOCKS):
        own = slice(i * BINS, (i + 1) * BINS)
        rows.append(jnp.sum(member[own] * (running + counts[own, 0:128]), axis=0, keepdims=True) - 1.0)
        running = running + counts[own, 128:256]
    position = jnp.concatenate(rows + [jnp.zeros((128 - BLOCKS, 128), jnp.float32)], axis=0).T
    for i in range(BLOCKS):
        order[i * 128 : i * 128 + 128, :] = jnp.broadcast_to(position[:, i : i + 1], (128, 128))

    k_min = jnp.min(jnp.min(nodes[2], axis=0), axis=0, keepdims=True)
    k_max = jnp.max(jnp.max(nodes[2], axis=0), axis=0, keepdims=True)
    for step in (1, 2, 4, 8):
        k_min = jnp.minimum(k_min, pltpu.roll(k_min, step, 1))
        k_max = jnp.maximum(k_max, pltpu.roll(k_max, step, 1))
    wide_id = lax.broadcasted_iota(jnp.int32, (BINS, 256), 0).astype(jnp.float32)
    wide_total = jnp.concatenate([total, total], axis=1)
    start = jnp.sum(jnp.where(wide_id < bin_of(k_min - MARGIN), wide_total, 0.0), axis=0, keepdims=True)
    stop = jnp.sum(jnp.where(wide_id <= bin_of(k_max + MARGIN), wide_total, 0.0), axis=0, keepdims=True)
    begin = jnp.floor(start * (1.0 / 32.0))
    count = jnp.floor((jnp.maximum(stop - 32.0 * begin, 1.0) + (CHUNK - 1.0)) * (1.0 / CHUNK))
    edges[0:1, :] = begin.astype(jnp.int32)
    edges[1:2, :] = count.astype(jnp.int32)
    at_tile = lax.broadcasted_iota(jnp.int32, (1, 256), 1) % 16 == 15
    beyond = jnp.max(jnp.where(at_tile, count - 1.0, 0.0), axis=1, keepdims=True)
    edges[3:4, :] = jnp.broadcast_to(beyond, (1, 256)).astype(jnp.int32)
    edges[2:3, :] = jnp.floor(
        (jnp.sum(wide_total, axis=0, keepdims=True) + (PLACED - 1.0)) * (1.0 / PLACED)
    ).astype(jnp.int32)
    copy = pltpu.make_async_copy(edges, ends, arrived)
    copy.start()

    def split(i, carry):
        for half in range(2):
            value = g_ref[2 * i + half]
            motion = value[0:24]
            top = motion.astype(jnp.bfloat16).astype(jnp.float32)
            spot = value[24:32] * 0.25
            one = spot.astype(jnp.bfloat16).astype(jnp.float32)
            two = (spot - one).astype(jnp.bfloat16).astype(jnp.float32)
            three = spot - one - two
            parts[i, :, half * 128 : half * 128 + 128] = jnp.concatenate(
                [top, motion - top, one, two, three, jnp.zeros((8, 128), jnp.float32)], axis=0
            ).astype(jnp.bfloat16)
        return carry

    lax.fori_loop(0, BLOCKS // 2, split, 0)
    copy.wait()

    slot = lax.broadcasted_iota(jnp.int32, (1, 128), 1)

    def place_chunk(s, carry):
        sums = jnp.zeros((80, PLACED), jnp.float32)
        wanted = [(slot + (s * PLACED + 128 * half)).astype(jnp.float32) for half in range(2)]
        for i in range(BLOCKS // 2):
            at = order[i * 256 : i * 256 + 256, :]
            hit = jnp.concatenate([jnp.where(at == w, 1.0, 0.0) for w in wanted], axis=1)
            sums = sums + whole_dot(parts[i], hit.astype(jnp.bfloat16))
        short = sums[0:48]
        spot = (sums[48:56] + sums[56:64]) + sums[64:72]
        for half in range(2):
            lanes = slice(half * 128, half * 128 + 128)
            weights[2 * s + half] = short[:, lanes]
            piece = jnp.concatenate([spot[:, lanes], jnp.zeros((120, 128), jnp.float32)], axis=0).T
            at = pl.multiple_of(s * PLACED + half * 128, 128)
            for c in range(3):
                centres[c, pl.ds(at, 128), :] = jnp.broadcast_to(piece[:, c : c + 1], (128, 128))
        return carry

    lax.fori_loop(0, ends[2, 0], place_chunk, 0)

    behind = 2 * ends[2, 0]
    for half in range(2):
        weights[behind + half] = jnp.zeros((48, CHUNK), jnp.float32)
        for c in range(3):
            centres[c, pl.ds(pl.multiple_of((behind + half) * CHUNK, CHUNK), CHUNK), :] = jnp.zeros((CHUNK, 128), jnp.float32)
    lane = lax.broadcasted_iota(jnp.int32, (48, CHUNK), 1)

    def shift_chunk(chunk, carry):
        here, after = weights[chunk], weights[chunk + 1]
        windows[4 * chunk] = here.astype(jnp.bfloat16)
        for r in range(1, 4):
            back = CHUNK - 32 * r
            moved = jnp.where(lane < back, pltpu.roll(here, back, 1), pltpu.roll(after, back, 1))
            windows[4 * chunk + r] = moved.astype(jnp.bfloat16)
        return carry

    lax.fori_loop(0, behind + 1, shift_chunk, 0)

    def window(t, place):
        at = pl.multiple_of(place * 32, 32)
        spot = [centres[c, pl.ds(at, CHUNK), :] for c in range(3)]
        pieces = windows[place]
        tops, rests = [], []
        for p in range(2):
            square = None
            for c in range(3):
                gap = spot[c] - tiles[t, 2 * c + p : 2 * c + p + 1, :]
                square = gap * gap if square is None else square + gap * gap
            radius = square * lax.rsqrt(jnp.maximum(square, 1e-30))
            rest = jnp.maximum(1.0 - radius, 0.0)
            rest = rest * rest
            value = rest * rest * (4.0 * radius + 1.0)
            top = value.astype(jnp.bfloat16)
            tops.append(top)
            rests.append((value - top.astype(jnp.float32)).astype(jnp.bfloat16))
        full = whole_dot(pieces, jnp.concatenate(tops, axis=1))
        extra = whole_dot(pieces[0:32], jnp.concatenate(rests, axis=1))
        return full[0:24] + (full[24:48] + extra[0:24])

    def first_windows(group, carry):
        for k in range(GROUP):
            t = group * GROUP + k
            found[t] = window(t, ends[0, 16 * t + 15])
        return carry

    lax.fori_loop(0, 16 // GROUP, first_windows, 0)

    @pl.when(ends[3, 0] > 0)
    def _():
        def more_windows(t, carry):
            def one(k, carry):
                found[t] += window(t, ends[0, 16 * t + 15] + 4 * k)
                return carry

            return lax.fori_loop(1, ends[1, 16 * t + 15], one, carry)

        lax.fori_loop(0, 16, more_windows, 0)

    for p in range(2):
        for half in range(2):
            lanes = slice(half * 128, half * 128 + 128)
            rows = swap_blocks([found[8 * half + t, :, p * 128 : p * 128 + 128] for t in range(8)])
            for j in range(8):
                for c in range(3):
                    value = rows[j][c * 8 : c * 8 + 8]
                    into = pl.ds(c * 32 + p * 16 + half * 8 + j, 8, stride=96)
                    moved_ref[into, :] = value
                    deformed_ref[into, :] = value + strip[c, p, j : j + 1, lanes]
    keep.wait()


def evaluate(gathered, base_nodes):
    shape = jax.ShapeDtypeStruct((INST * 96, 128), jnp.float32)
    moved, deformed, kept = pl.pallas_call(
        evaluate_kernel,
        out_shape=(shape, shape, jax.ShapeDtypeStruct(base_nodes.shape, jnp.float32)),
        in_specs=[vmem()] * 2,
        out_specs=(vmem(), vmem(), vmem()),
        scratch_shapes=[
            pltpu.VMEM((3, 2, 8, 256), jnp.float32),
            pltpu.VMEM((16, 8, 128), jnp.float32),
            pltpu.VMEM((3, 2, 8, 256), jnp.float32),
            pltpu.VMEM((BLOCKS // 2, 80, 256), jnp.bfloat16),
            pltpu.VMEM((NC, 128), jnp.float32),
            pltpu.VMEM((NC // CHUNK + 2, 48, CHUNK), jnp.float32),
            pltpu.VMEM((4 * (NC // CHUNK + 1), 48, CHUNK), jnp.bfloat16),
            pltpu.VMEM((3, NC + 2 * CHUNK, 128), jnp.float32),
            pltpu.VMEM((16, 24, 256), jnp.float32),
            pltpu.VMEM((8, 256), jnp.int32),
            pltpu.SMEM((8, 256), jnp.int32),
            pltpu.SemaphoreType.DMA,
            pltpu.SemaphoreType.DMA,
        ],
        compiler_params=params(),
        name="evaluate",
    )(gathered, base_nodes)
    shape = (INST, 3, 2, 2, 8, 128)
    return moved.reshape(shape), deformed.reshape(shape), kept


def exchange_kernel(moved_ref, deformed_ref, own, halo, send, recv, local):
    inst, space = lax.axis_index("inst"), lax.axis_index("space")
    behind, ahead = lax.rem(space + SPACE - 1, SPACE), lax.rem(space + 1, SPACE)
    barrier = pltpu.get_barrier_semaphore()
    targets = [lax.rem(inst + k, INST) for k in range(INST)]
    peers = [(t, s) for t in targets for s in (behind, ahead)] + [(t, space) for t in targets[1:]]
    for peer in peers:
        pl.semaphore_signal(barrier, inc=1, device_id=peer, device_id_type=MESH)
    rows = pl.ds(pl.multiple_of(inst * 8, 8), 8)
    stays = pltpu.make_async_copy(moved_ref.at[inst], own.at[:, :, :, rows, :], local)
    stays.start()
    pl.semaphore_wait(barrier, len(peers))
    copies = []

    def start(source, target, kind, k, device):
        copy = pltpu.make_async_remote_copy(
            src_ref=source,
            dst_ref=target,
            send_sem=send.at[kind, k],
            recv_sem=recv.at[kind, k],
            device_id=device,
            device_id_type=MESH,
        )
        copy.start()
        copies.append(copy)

    for k in (4, 3, 5, 2, 6, 1, 7, 0):
        t = targets[k]
        start(deformed_ref.at[t, :, 0], halo.at[1, :, :, rows, :], 0, k, (t, behind))
        start(deformed_ref.at[t, :, 1], halo.at[0, :, :, rows, :], 1, k, (t, ahead))
        if k:
            start(moved_ref.at[t], own.at[:, :, :, rows, :], 2, k, (t, space))
    for copy in [stays] + copies:
        copy.wait()


def exchange(moved, deformed, rows, width):
    return pl.pallas_call(
        exchange_kernel,
        out_shape=(
            jax.ShapeDtypeStruct((3, 2, 2, rows, width), jnp.float32),
            jax.ShapeDtypeStruct((2, 3, 2, rows, width), jnp.float32),
        ),
        in_specs=[vmem(), vmem()],
        out_specs=(vmem(), vmem()),
        scratch_shapes=[
            pltpu.SemaphoreType.DMA((3, INST)),
            pltpu.SemaphoreType.DMA((3, INST)),
            pltpu.SemaphoreType.DMA,
        ],
        compiler_params=params(collective_id=1, has_side_effects=True),
        name="exchange",
    )(moved, deformed)


def shifted(value, axis):
    extent = value.shape[axis]
    at = lax.broadcasted_iota(jnp.int32, value.shape, axis)
    following = pltpu.roll(value, extent - 1, axis)
    preceding = pltpu.roll(value, 1, axis)
    upper = jnp.where(at == extent - 1, 2.0 * value - preceding, following)
    lower = jnp.where(at == 0, 2.0 * value - following, preceding)
    return (upper - lower) * 0.5


def cross(a, b):
    return [
        a[1] * b[2] - a[2] * b[1],
        a[2] * b[0] - a[0] * b[2],
        a[0] * b[1] - a[1] * b[0],
    ]


def metrics_kernel(own, halo, n_ref, disp_hbm, metrics_hbm, disp, metrics, sems):
    space = lax.axis_index("space")
    copies = []

    def leave(source, target):
        copy = pltpu.make_async_copy(source, target, sems.at[len(copies)])
        copy.start()
        copies.append(copy)

    for c in range(3):
        for p in range(2):
            for half in range(2):
                disp[c, p, :, half * 128 : half * 128 + 128] = own[c, p, half]
    leave(disp, disp_hbm.at[0])

    def beside(which, c):
        return jnp.concatenate([halo[which, c, 0], halo[which, c, 1]], axis=1)

    for p in range(2):
        here = [n_ref[c, p] + disp[c, p] for c in range(3)]
        there = [n_ref[c, 1 - p] + disp[c, 1 - p] for c in range(3)]
        along_i = []
        for c in range(3):
            if p == 0:
                beyond = jnp.where(space == 0, 2.0 * here[c] - there[c], beside(0, c))
                along_i.append((there[c] - beyond) * 0.5)
            else:
                beyond = jnp.where(space == SPACE - 1, 2.0 * here[c] - there[c], beside(1, c))
                along_i.append((beyond - there[c]) * 0.5)
        along_j = [shifted(value, 0) for value in here]
        along_k = [shifted(value, 1) for value in here]
        one = cross(along_j, along_k)
        two = cross(along_k, along_i)
        three = cross(along_i, along_j)
        last = along_i[0] * one[0] + along_i[1] * one[1] + along_i[2] * one[2]
        for row, value in enumerate(one + two + three + [last]):
            metrics[p, row] = value
        leave(metrics.at[p], metrics_hbm.at[0, :, p])
    for copy in copies:
        copy.wait()


def metric_rows(own, halo, base_nodes):
    anywhere = pl.BlockSpec(memory_space=pltpu.HBM)
    return pl.pallas_call(
        metrics_kernel,
        out_shape=(
            jax.ShapeDtypeStruct((1,) + base_nodes.shape, jnp.float32),
            jax.ShapeDtypeStruct((1, 10) + base_nodes.shape[1:], jnp.float32),
        ),
        in_specs=[vmem()] * 3,
        out_specs=(anywhere, anywhere),
        scratch_shapes=[
            pltpu.VMEM(base_nodes.shape, jnp.float32),
            pltpu.VMEM((2, 10) + base_nodes.shape[2:], jnp.float32),
            pltpu.SemaphoreType.DMA((3,)),
        ],
        compiler_params=params(),
        name="metrics",
    )(own, halo, base_nodes)


def body(amplitudes, modal_coeffs, centre_positions, base_nodes):
    modes = amplitudes.shape[1]
    own = jnp.concatenate(
        [
            modal_coeffs.transpose(1, 2, 0).reshape(3 * OWN, modes),
            amplitudes,
            jnp.pad(centre_positions, ((0, 5), (0, modes - OWN))),
        ],
        axis=0,
    )
    gathered = gather(own)
    moved, deformed, nodes = evaluate(gathered, base_nodes)
    rows, width = base_nodes.shape[2], base_nodes.shape[3] // 2
    own, halo = exchange(moved, deformed, rows, width)
    return metric_rows(own, halo, nodes)


def solution(mesh):
    in_specs = (
        P(),
        P(None, None, ("inst", "space")),
        P(None, ("inst", "space")),
        P(None, "space", None, None),
    )
    out_specs = (P("inst", None, "space", None, None), P("inst", None, "space", None, None))
    return jax.shard_map(body, mesh=mesh, in_specs=in_specs, out_specs=out_specs, check_vma=False)
```

```python
import jax
import jax.numpy as jnp
from jax import lax
from jax.experimental import pallas as pl
from jax.experimental.pallas import tpu as pltpu
from jax.sharding import PartitionSpec as P

MESH = pl.DeviceIdType.MESH
HIGH = lax.Precision.HIGHEST
XS, YS, ZS, CORES = 4, 4, 16, 2
INST, SPACE = YS * CORES, XS * ZS
OWN = 8
BLOCKS = XS * YS * CORES
NC = BLOCKS * ZS * OWN
VALUES = 32
BINS = 32
CHUNK = 128
GROUP = 8
PLACED = 256
MARGIN = 1.0 + 2.0**-11
VMEM_LIMIT = 48 * 1024 * 1024


def vmem():
    return pl.BlockSpec(memory_space=pltpu.VMEM)


def params(**more):
    return pltpu.CompilerParams(vmem_limit_bytes=VMEM_LIMIT, **more)


def swap_blocks(arrays):
    block = lax.broadcasted_iota(jnp.int32, arrays[0].shape, 1) // 16
    arrays = list(arrays)
    for step in (1, 2, 4):
        upper = (block & step) != 0
        for a in range(8):
            if not a & step:
                one, two = arrays[a], arrays[a | step]
                arrays[a] = jnp.where(upper, pltpu.roll(two, 16 * step, 1), one)
                arrays[a | step] = jnp.where(upper, two, pltpu.roll(one, 128 - 16 * step, 1))
    return arrays


def gather_kernel(own_ref, out_ref, zbuf, send, recv):
    inst, space = lax.axis_index("inst"), lax.axis_index("space")
    y, core = inst // CORES, inst % CORES
    x, z = space // ZS, space % ZS
    z_peers = [(inst, x * ZS + lax.rem(z + k, ZS)) for k in range(1, ZS)]
    steps = [(a, b) for a in range(YS) for b in range(XS) if a or b]
    plane_peers = [
        (lax.rem(y + a, YS) * CORES + core, lax.rem(x + b, XS) * ZS + z) for a, b in steps
    ]
    other = (y * CORES + (1 - core), space)

    def hops(a, b, c):
        return min(a, ZS - a) + min(b, YS - b) + min(c, XS - c)

    z_order = sorted(range(ZS - 1), key=lambda k: -hops(k + 1, 0, 0))
    plane_order = sorted(range(len(steps)), key=lambda k: -hops(0, *steps[k]))
    peers = [z_peers[k] for k in z_order] + [plane_peers[k] for k in plane_order] + [other]
    barrier = pltpu.get_barrier_semaphore()
    for peer in peers:
        pl.semaphore_signal(barrier, inc=1, device_id=peer, device_id_type=MESH)

    transposed = (((1,), (1,)), ((), ()))

    def high_dot(a, b):
        return lax.dot_general(a, b, transposed, precision=HIGH, preferred_element_type=jnp.float32)

    amp = own_ref[24:32]
    eye = (
        lax.broadcasted_iota(jnp.int32, (OWN, OWN), 0) == lax.broadcasted_iota(jnp.int32, (OWN, OWN), 1)
    ).astype(jnp.float32)
    own = [high_dot(own_ref[8 * c : 8 * c + 8], amp) for c in range(3)]
    own.append(high_dot(eye, own_ref[32:40, 0:OWN])[:, 0:3])
    own = jnp.concatenate(own + [jnp.zeros((OWN, 128 - 27), jnp.float32)], axis=1)
    row_id = lax.broadcasted_iota(jnp.int32, (OWN, 128), 0) % 4
    spread = jnp.zeros((OWN, 128), jnp.float32)
    for a in range(4):
        moved = own if a == 0 else pltpu.roll(own, VALUES * a, 1)
        spread = spread + jnp.where(row_id == a, moved, 0.0)
    zbuf[z] = jnp.concatenate(
        [
            jnp.sum(spread[0:4], axis=0, keepdims=True),
            jnp.sum(spread[4:8], axis=0, keepdims=True),
        ],
        axis=0,
    )

    pl.semaphore_wait(barrier, len(peers))

    def start(ref, k, peer):
        copy = pltpu.make_async_remote_copy(
            src_ref=ref,
            dst_ref=ref,
            send_sem=send.at[k],
            recv_sem=recv.at[k],
            device_id=peer,
            device_id_type=MESH,
        )
        copy.start()
        return copy

    copies = [start(zbuf.at[z], k, z_peers[k]) for k in z_order]
    for copy in reversed(copies):
        copy.wait()
    rows = jnp.concatenate([zbuf[i] for i in range(ZS)], axis=0)
    rows = jnp.concatenate([rows, jnp.zeros((128 - 2 * ZS, 128), jnp.float32)], axis=0).T
    block = rows[0:VALUES]
    for a in range(1, 4):
        block = block + pltpu.roll(rows[VALUES * a : VALUES * (a + 1)], VALUES * a, 1)
    mine = core * (XS * YS) + y * XS + x
    out_ref[mine] = block

    copies = [start(out_ref.at[mine], ZS - 1 + k, plane_peers[k]) for k in plane_order]
    passed = [start(out_ref.at[mine], ZS - 1 + len(steps), other)]
    for copy, k in reversed(list(zip(copies, plane_order))):
        copy.wait_recv()
        a, b = steps[k]
        origin = core * (XS * YS) + lax.rem(y + YS - a, YS) * XS + lax.rem(x + XS - b, XS)
        passed.append(start(out_ref.at[origin], ZS + len(steps) + k, other))
    for copy in copies:
        copy.wait_send()
    for copy in passed:
        copy.wait()


def gather(own):
    count = ZS + 2 * XS * YS - 2
    return pl.pallas_call(
        gather_kernel,
        out_shape=jax.ShapeDtypeStruct((BLOCKS, VALUES, 128), jnp.float32),
        in_specs=[vmem()],
        out_specs=vmem(),
        scratch_shapes=[
            pltpu.VMEM((ZS, 2, 128), jnp.float32),
            pltpu.SemaphoreType.DMA((count,)),
            pltpu.SemaphoreType.DMA((count,)),
        ],
        compiler_params=params(collective_id=0, has_side_effects=True),
        cost_estimate=pl.CostEstimate(flops=10**9, bytes_accessed=2 * 10**7, transcendentals=0),
        name="gather",
    )(own)


def whole_dot(a, b, precision=None):
    return jnp.dot(a, b, precision=precision, preferred_element_type=jnp.float32)


def evaluate_kernel(g_ref, n_ref, moved_ref, kept, tiles, nodes, parts, order, weights, windows, centres, found, edges, ends, arrived, passing):
    keep = pltpu.make_async_copy(n_ref, kept, passing)
    keep.start()
    first = pl.multiple_of(lax.axis_index("inst") * 8, 8)
    nodes[...] = n_ref[:, :, pl.ds(first, 8), :] * 0.25

    for half in range(2):
        lanes = slice(half * 128, half * 128 + 128)
        rows = [
            jnp.concatenate(
                [nodes[c, p, j : j + 1, lanes] for c in range(3) for p in range(2)]
                + [jnp.zeros((2, 128), jnp.float32)],
                axis=0,
            )
            for j in range(8)
        ]
        for t, tile in enumerate(swap_blocks(rows)):
            tiles[8 * half + t] = tile
    spots = [g_ref[:, 24 + c, :] * 0.25 for c in range(3)]
    near = None
    for c in range(3):
        low = jnp.min(nodes[c]) - MARGIN
        high = jnp.max(nodes[c]) + MARGIN
        inside = (spots[c] >= low) & (spots[c] <= high)
        near = inside if near is None else near & inside
        if c == 2:
            k_low, scale = low, BINS / jnp.full((1, 1), high - low)

    def bin_of(value):
        return jnp.clip(jnp.floor((value - k_low) * scale), 0.0, BINS - 1.0)

    bins = jnp.where(near, bin_of(spots[2]), -1.0)

    bin_id = lax.broadcasted_iota(jnp.int32, (BINS, 128), 0).astype(jnp.float32)
    member = jnp.concatenate(
        [(bins[i : i + 1] == bin_id).astype(jnp.float32) for i in range(BLOCKS)], axis=0
    )
    lane = lax.broadcasted_iota(jnp.int32, (128, 256), 1)
    counting = ((lax.broadcasted_iota(jnp.int32, (128, 256), 0) <= lane) | (lane >= 128)).astype(jnp.float32)
    counts = whole_dot(member.astype(jnp.bfloat16), counting.astype(jnp.bfloat16))
    total = counts[0:BINS, 128:256]
    for i in range(1, BLOCKS):
        total = total + counts[i * BINS : (i + 1) * BINS, 128:256]
    earlier = (
        lax.broadcasted_iota(jnp.int32, (BINS, BINS), 1) < lax.broadcasted_iota(jnp.int32, (BINS, BINS), 0)
    ).astype(jnp.float32)
    running = whole_dot(earlier, total, HIGH)
    rows = []
    for i in range(BLOCKS):
        own = slice(i * BINS, (i + 1) * BINS)
        rows.append(jnp.sum(member[own] * (running + counts[own, 0:128]), axis=0, keepdims=True) - 1.0)
        running = running + counts[own, 128:256]
    position = jnp.concatenate(rows + [jnp.zeros((128 - BLOCKS, 128), jnp.float32)], axis=0).T
    for i in range(BLOCKS):
        order[i * 128 : i * 128 + 128, :] = jnp.broadcast_to(position[:, i : i + 1], (128, 128))

    k_min = jnp.min(jnp.min(nodes[2], axis=0), axis=0, keepdims=True)
    k_max = jnp.max(jnp.max(nodes[2], axis=0), axis=0, keepdims=True)
    for step in (1, 2, 4, 8):
        k_min = jnp.minimum(k_min, pltpu.roll(k_min, step, 1))
        k_max = jnp.maximum(k_max, pltpu.roll(k_max, step, 1))
    wide_id = lax.broadcasted_iota(jnp.int32, (BINS, 256), 0).astype(jnp.float32)
    wide_total = jnp.concatenate([total, total], axis=1)
    start = jnp.sum(jnp.where(wide_id < bin_of(k_min - MARGIN), wide_total, 0.0), axis=0, keepdims=True)
    stop = jnp.sum(jnp.where(wide_id <= bin_of(k_max + MARGIN), wide_total, 0.0), axis=0, keepdims=True)
    begin = jnp.floor(start * (1.0 / 32.0))
    count = jnp.floor((jnp.maximum(stop - 32.0 * begin, 1.0) + (CHUNK - 1.0)) * (1.0 / CHUNK))
    edges[0:1, :] = begin.astype(jnp.int32)
    edges[1:2, :] = count.astype(jnp.int32)
    at_tile = lax.broadcasted_iota(jnp.int32, (1, 256), 1) % 16 == 15
    beyond = jnp.max(jnp.where(at_tile, count - 1.0, 0.0), axis=1, keepdims=True)
    edges[3:4, :] = jnp.broadcast_to(beyond, (1, 256)).astype(jnp.int32)
    edges[2:3, :] = jnp.floor(
        (jnp.sum(wide_total, axis=0, keepdims=True) + (PLACED - 1.0)) * (1.0 / PLACED)
    ).astype(jnp.int32)
    copy = pltpu.make_async_copy(edges, ends, arrived)
    copy.start()

    def split(i, carry):
        for half in range(2):
            value = g_ref[2 * i + half]
            motion = value[0:24]
            top = motion.astype(jnp.bfloat16).astype(jnp.float32)
            spot = value[24:32] * 0.25
            one = spot.astype(jnp.bfloat16).astype(jnp.float32)
            two = (spot - one).astype(jnp.bfloat16).astype(jnp.float32)
            three = spot - one - two
            parts[i, :, half * 128 : half * 128 + 128] = jnp.concatenate(
                [top, motion - top, one, two, three, jnp.zeros((8, 128), jnp.float32)], axis=0
            ).astype(jnp.bfloat16)
        return carry

    lax.fori_loop(0, BLOCKS // 2, split, 0)
    copy.wait()

    slot = lax.broadcasted_iota(jnp.int32, (1, 128), 1)

    def place_chunk(s, carry):
        sums = jnp.zeros((80, PLACED), jnp.float32)
        wanted = [(slot + (s * PLACED + 128 * half)).astype(jnp.float32) for half in range(2)]
        for i in range(BLOCKS // 2):
            at = order[i * 256 : i * 256 + 256, :]
            hit = jnp.concatenate([jnp.where(at == w, 1.0, 0.0) for w in wanted], axis=1)
            sums = sums + whole_dot(parts[i], hit.astype(jnp.bfloat16))
        short = sums[0:48]
        spot = (sums[48:56] + sums[56:64]) + sums[64:72]
        for half in range(2):
            lanes = slice(half * 128, half * 128 + 128)
            weights[2 * s + half] = short[:, lanes]
            piece = jnp.concatenate([spot[:, lanes], jnp.zeros((120, 128), jnp.float32)], axis=0).T
            at = pl.multiple_of(s * PLACED + half * 128, 128)
            for c in range(3):
                centres[c, pl.ds(at, 128), :] = jnp.broadcast_to(piece[:, c : c + 1], (128, 128))
        return carry

    lax.fori_loop(0, ends[2, 0], place_chunk, 0)

    behind = 2 * ends[2, 0]
    for half in range(2):
        weights[behind + half] = jnp.zeros((48, CHUNK), jnp.float32)
        for c in range(3):
            centres[c, pl.ds(pl.multiple_of((behind + half) * CHUNK, CHUNK), CHUNK), :] = jnp.zeros((CHUNK, 128), jnp.float32)
    lane = lax.broadcasted_iota(jnp.int32, (48, CHUNK), 1)

    def shift_chunk(chunk, carry):
        here, after = weights[chunk], weights[chunk + 1]
        windows[4 * chunk] = here.astype(jnp.bfloat16)
        for r in range(1, 4):
            back = CHUNK - 32 * r
            moved = jnp.where(lane < back, pltpu.roll(here, back, 1), pltpu.roll(after, back, 1))
            windows[4 * chunk + r] = moved.astype(jnp.bfloat16)
        return carry

    lax.fori_loop(0, behind + 1, shift_chunk, 0)

    def window(t, place):
        at = pl.multiple_of(place * 32, 32)
        spot = [centres[c, pl.ds(at, CHUNK), :] for c in range(3)]
        pieces = windows[place]
        tops, rests = [], []
        for p in range(2):
            square = None
            for c in range(3):
                gap = spot[c] - tiles[t, 2 * c + p : 2 * c + p + 1, :]
                square = gap * gap if square is None else square + gap * gap
            radius = square * lax.rsqrt(jnp.maximum(square, 1e-30))
            rest = jnp.maximum(1.0 - radius, 0.0)
            rest = rest * rest
            value = rest * rest * (4.0 * radius + 1.0)
            top = value.astype(jnp.bfloat16)
            tops.append(top)
            rests.append((value - top.astype(jnp.float32)).astype(jnp.bfloat16))
        full = whole_dot(pieces, jnp.concatenate(tops, axis=1))
        extra = whole_dot(pieces[0:32], jnp.concatenate(rests, axis=1))
        return full[0:24] + (full[24:48] + extra[0:24])

    def first_windows(group, carry):
        for k in range(GROUP):
            t = group * GROUP + k
            found[t] = window(t, ends[0, 16 * t + 15])
        return carry

    lax.fori_loop(0, 16 // GROUP, first_windows, 0)

    @pl.when(ends[3, 0] > 0)
    def _():
        def more_windows(t, carry):
            def one(k, carry):
                found[t] += window(t, ends[0, 16 * t + 15] + 4 * k)
                return carry

            return lax.fori_loop(1, ends[1, 16 * t + 15], one, carry)

        lax.fori_loop(0, 16, more_windows, 0)

    for p in range(2):
        for half in range(2):
            rows = swap_blocks([found[8 * half + t, :, p * 128 : p * 128 + 128] for t in range(8)])
            for j in range(8):
                for c in range(3):
                    into = pl.ds(c * 32 + p * 16 + half * 8 + j, 8, stride=96)
                    moved_ref[into, :] = rows[j][c * 8 : c * 8 + 8]
    keep.wait()


def evaluate(gathered, base_nodes):
    shape = jax.ShapeDtypeStruct((INST * 96, 128), jnp.float32)
    moved, kept = pl.pallas_call(
        evaluate_kernel,
        out_shape=(shape, jax.ShapeDtypeStruct(base_nodes.shape, jnp.float32)),
        in_specs=[vmem()] * 2,
        out_specs=(vmem(), vmem()),
        scratch_shapes=[
            pltpu.VMEM((16, 8, 128), jnp.float32),
            pltpu.VMEM((3, 2, 8, 256), jnp.float32),
            pltpu.VMEM((BLOCKS // 2, 80, 256), jnp.bfloat16),
            pltpu.VMEM((NC, 128), jnp.float32),
            pltpu.VMEM((NC // CHUNK + 2, 48, CHUNK), jnp.float32),
            pltpu.VMEM((4 * (NC // CHUNK + 1), 48, CHUNK), jnp.bfloat16),
            pltpu.VMEM((3, NC + 2 * CHUNK, 128), jnp.float32),
            pltpu.VMEM((16, 24, 256), jnp.float32),
            pltpu.VMEM((8, 256), jnp.int32),
            pltpu.SMEM((8, 256), jnp.int32),
            pltpu.SemaphoreType.DMA,
            pltpu.SemaphoreType.DMA,
        ],
        compiler_params=params(),
        name="evaluate",
    )(gathered, base_nodes)
    return moved.reshape(INST, 3, 2, 2, 8, 128), kept


def exchange_kernel(moved_ref, n_ref, own, halo, deformed, send, recv, send_on, recv_on):
    inst, space = lax.axis_index("inst"), lax.axis_index("space")
    behind, ahead = lax.rem(space + SPACE - 1, SPACE), lax.rem(space + 1, SPACE)
    order = (4, 3, 5, 2, 6, 1, 7)
    peers = [(lax.rem(inst + k, INST), space) for k in order] + [(inst, behind), (inst, ahead)]
    barrier = pltpu.get_barrier_semaphore()
    for peer in peers:
        pl.semaphore_signal(barrier, inc=1, device_id=peer, device_id_type=MESH)

    def start(source, target, sent, arrived, device):
        copy = pltpu.make_async_remote_copy(
            src_ref=source,
            dst_ref=target,
            send_sem=sent,
            recv_sem=arrived,
            device_id=device,
            device_id_type=MESH,
        )
        copy.start()
        return copy

    def rows_of(strip):
        return pl.ds(pl.multiple_of(strip * 8, 8), 8)

    def add_nodes(rows):
        for c in range(3):
            for p in range(2):
                nodes = n_ref[c, p, rows, :]
                for half in range(2):
                    lanes = slice(half * 128, half * 128 + 128)
                    deformed[p, c, half, rows, :] = own[c, p, half, rows, :] + nodes[:, lanes]

    def pass_on(k, rows):
        return [
            start(
                deformed.at[side, :, :, rows, :],
                halo.at[1 - side, :, :, rows, :],
                send_on.at[side, k],
                recv_on.at[side, k],
                (inst, (behind, ahead)[side]),
            )
            for side in range(2)
        ]

    mine = rows_of(inst)
    own[:, :, :, mine, :] = moved_ref[inst]
    add_nodes(mine)
    pl.semaphore_wait(barrier, len(peers))
    copies = [
        start(moved_ref.at[peer[0]], own.at[:, :, :, mine, :], send.at[k], recv.at[k], peer)
        for k, peer in zip(order, peers)
    ]
    passed = pass_on(0, mine)
    for k, copy in reversed(list(zip(order, copies))):
        copy.wait_recv()
        rows = rows_of(lax.rem(inst + INST - k, INST))
        add_nodes(rows)
        passed += pass_on(k, rows)
    for copy in copies:
        copy.wait_send()
    for copy in passed:
        copy.wait()


def exchange(moved, base_nodes):
    rows, width = base_nodes.shape[2], base_nodes.shape[3] // 2
    return pl.pallas_call(
        exchange_kernel,
        out_shape=(
            jax.ShapeDtypeStruct((3, 2, 2, rows, width), jnp.float32),
            jax.ShapeDtypeStruct((2, 3, 2, rows, width), jnp.float32),
        ),
        in_specs=[vmem(), vmem()],
        out_specs=(vmem(), vmem()),
        scratch_shapes=[
            pltpu.VMEM((2, 3, 2, rows, width), jnp.float32),
            pltpu.SemaphoreType.DMA((INST,)),
            pltpu.SemaphoreType.DMA((INST,)),
            pltpu.SemaphoreType.DMA((2, INST)),
            pltpu.SemaphoreType.DMA((2, INST)),
        ],
        compiler_params=params(collective_id=1, has_side_effects=True),
        name="exchange",
    )(moved, base_nodes)


def shifted(value, axis):
    extent = value.shape[axis]
    at = lax.broadcasted_iota(jnp.int32, value.shape, axis)
    following = pltpu.roll(value, extent - 1, axis)
    preceding = pltpu.roll(value, 1, axis)
    upper = jnp.where(at == extent - 1, 2.0 * value - preceding, following)
    lower = jnp.where(at == 0, 2.0 * value - following, preceding)
    return (upper - lower) * 0.5


def cross(a, b):
    return [
        a[1] * b[2] - a[2] * b[1],
        a[2] * b[0] - a[0] * b[2],
        a[0] * b[1] - a[1] * b[0],
    ]


def metrics_kernel(own, halo, n_ref, disp_hbm, metrics_hbm, disp, metrics, sems):
    space = lax.axis_index("space")
    copies = []

    def leave(source, target):
        copy = pltpu.make_async_copy(source, target, sems.at[len(copies)])
        copy.start()
        copies.append(copy)

    for c in range(3):
        for p in range(2):
            for half in range(2):
                disp[c, p, :, half * 128 : half * 128 + 128] = own[c, p, half]
    leave(disp, disp_hbm.at[0])

    def beside(which, c):
        return jnp.concatenate([halo[which, c, 0], halo[which, c, 1]], axis=1)

    for p in range(2):
        here = [n_ref[c, p] + disp[c, p] for c in range(3)]
        there = [n_ref[c, 1 - p] + disp[c, 1 - p] for c in range(3)]
        along_i = []
        for c in range(3):
            if p == 0:
                beyond = jnp.where(space == 0, 2.0 * here[c] - there[c], beside(0, c))
                along_i.append((there[c] - beyond) * 0.5)
            else:
                beyond = jnp.where(space == SPACE - 1, 2.0 * here[c] - there[c], beside(1, c))
                along_i.append((beyond - there[c]) * 0.5)
        along_j = [shifted(value, 0) for value in here]
        along_k = [shifted(value, 1) for value in here]
        one = cross(along_j, along_k)
        two = cross(along_k, along_i)
        three = cross(along_i, along_j)
        last = along_i[0] * one[0] + along_i[1] * one[1] + along_i[2] * one[2]
        for row, value in enumerate(one + two + three + [last]):
            metrics[p, row] = value
        leave(metrics.at[p], metrics_hbm.at[0, :, p])
    for copy in copies:
        copy.wait()


def metric_rows(own, halo, base_nodes):
    anywhere = pl.BlockSpec(memory_space=pltpu.HBM)
    return pl.pallas_call(
        metrics_kernel,
        out_shape=(
            jax.ShapeDtypeStruct((1,) + base_nodes.shape, jnp.float32),
            jax.ShapeDtypeStruct((1, 10) + base_nodes.shape[1:], jnp.float32),
        ),
        in_specs=[vmem()] * 3,
        out_specs=(anywhere, anywhere),
        scratch_shapes=[
            pltpu.VMEM(base_nodes.shape, jnp.float32),
            pltpu.VMEM((2, 10) + base_nodes.shape[2:], jnp.float32),
            pltpu.SemaphoreType.DMA((3,)),
        ],
        compiler_params=params(),
        name="metrics",
    )(own, halo, base_nodes)


def body(amplitudes, modal_coeffs, centre_positions, base_nodes):
    modes = amplitudes.shape[1]
    own = jnp.concatenate(
        [
            modal_coeffs.transpose(1, 2, 0).reshape(3 * OWN, modes),
            amplitudes,
            jnp.pad(centre_positions, ((0, 5), (0, modes - OWN))),
        ],
        axis=0,
    )
    gathered = gather(own)
    moved, nodes = evaluate(gathered, base_nodes)
    own, halo = exchange(moved, nodes)
    return metric_rows(own, halo, nodes)


def solution(mesh):
    in_specs = (
        P(),
        P(None, None, ("inst", "space")),
        P(None, ("inst", "space")),
        P(None, "space", None, None),
    )
    out_specs = (P("inst", None, "space", None, None), P("inst", None, "space", None, None))
    return jax.shard_map(body, mesh=mesh, in_specs=in_specs, out_specs=out_specs, check_vma=False)
```

```python
import jax
import jax.numpy as jnp
from jax import lax
from jax.experimental import pallas as pl
from jax.experimental.pallas import tpu as pltpu
from jax.sharding import PartitionSpec as P

MESH = pl.DeviceIdType.MESH
HIGH = lax.Precision.HIGHEST
XS, YS, ZS, CORES = 4, 4, 16, 2
INST, SPACE = YS * CORES, XS * ZS
OWN = 8
BLOCKS = XS * YS * CORES
NC = BLOCKS * ZS * OWN
VALUES = 32
BINS = 32
CHUNK = 128
GROUP = 8
PLACED = 256
MARGIN = 1.0 + 2.0**-11
VMEM_LIMIT = 48 * 1024 * 1024


def vmem():
    return pl.BlockSpec(memory_space=pltpu.VMEM)


def params(**more):
    return pltpu.CompilerParams(vmem_limit_bytes=VMEM_LIMIT, **more)


def swap_blocks(arrays):
    block = lax.broadcasted_iota(jnp.int32, arrays[0].shape, 1) // 16
    arrays = list(arrays)
    for step in (1, 2, 4):
        upper = (block & step) != 0
        for a in range(8):
            if not a & step:
                one, two = arrays[a], arrays[a | step]
                arrays[a] = jnp.where(upper, pltpu.roll(two, 16 * step, 1), one)
                arrays[a | step] = jnp.where(upper, two, pltpu.roll(one, 128 - 16 * step, 1))
    return arrays


def gather_kernel(own_ref, out_ref, zbuf, send, recv):
    inst, space = lax.axis_index("inst"), lax.axis_index("space")
    y, core = inst // CORES, inst % CORES
    x, z = space // ZS, space % ZS
    z_peers = [(inst, x * ZS + lax.rem(z + k, ZS)) for k in range(1, ZS)]
    steps = [(a, b) for a in range(YS) for b in range(XS) if a or b]
    plane_peers = [
        (lax.rem(y + a, YS) * CORES + core, lax.rem(x + b, XS) * ZS + z) for a, b in steps
    ]
    other = (y * CORES + (1 - core), space)

    def hops(a, b, c):
        return min(a, ZS - a) + min(b, YS - b) + min(c, XS - c)

    z_order = sorted(range(ZS - 1), key=lambda k: -hops(k + 1, 0, 0))
    plane_order = sorted(range(len(steps)), key=lambda k: -hops(0, *steps[k]))
    peers = [z_peers[k] for k in z_order] + [plane_peers[k] for k in plane_order] + [other]
    barrier = pltpu.get_barrier_semaphore()
    for peer in peers:
        pl.semaphore_signal(barrier, inc=1, device_id=peer, device_id_type=MESH)

    transposed = (((1,), (1,)), ((), ()))

    def high_dot(a, b):
        return lax.dot_general(a, b, transposed, precision=HIGH, preferred_element_type=jnp.float32)

    amp = own_ref[24:32]
    eye = (
        lax.broadcasted_iota(jnp.int32, (OWN, OWN), 0) == lax.broadcasted_iota(jnp.int32, (OWN, OWN), 1)
    ).astype(jnp.float32)
    own = [high_dot(own_ref[8 * c : 8 * c + 8], amp) for c in range(3)]
    own.append(high_dot(eye, own_ref[32:40, 0:OWN])[:, 0:3])
    own = jnp.concatenate(own + [jnp.zeros((OWN, 128 - 27), jnp.float32)], axis=1)
    row_id = lax.broadcasted_iota(jnp.int32, (OWN, 128), 0) % 4
    spread = jnp.zeros((OWN, 128), jnp.float32)
    for a in range(4):
        moved = own if a == 0 else pltpu.roll(own, VALUES * a, 1)
        spread = spread + jnp.where(row_id == a, moved, 0.0)
    zbuf[z] = jnp.concatenate(
        [
            jnp.sum(spread[0:4], axis=0, keepdims=True),
            jnp.sum(spread[4:8], axis=0, keepdims=True),
        ],
        axis=0,
    )

    pl.semaphore_wait(barrier, len(peers))

    def start(ref, k, peer):
        copy = pltpu.make_async_remote_copy(
            src_ref=ref,
            dst_ref=ref,
            send_sem=send.at[k],
            recv_sem=recv.at[k],
            device_id=peer,
            device_id_type=MESH,
        )
        copy.start()
        return copy

    copies = [start(zbuf.at[z], k, z_peers[k]) for k in z_order]
    for copy in reversed(copies):
        copy.wait()
    rows = jnp.concatenate([zbuf[i] for i in range(ZS)], axis=0)
    rows = jnp.concatenate([rows, jnp.zeros((128 - 2 * ZS, 128), jnp.float32)], axis=0).T
    block = rows[0:VALUES]
    for a in range(1, 4):
        block = block + pltpu.roll(rows[VALUES * a : VALUES * (a + 1)], VALUES * a, 1)
    mine = core * (XS * YS) + y * XS + x
    out_ref[mine] = block

    copies = [start(out_ref.at[mine], ZS - 1 + k, plane_peers[k]) for k in plane_order]
    passed = [start(out_ref.at[mine], ZS - 1 + len(steps), other)]
    for copy, k in reversed(list(zip(copies, plane_order))):
        copy.wait_recv()
        a, b = steps[k]
        origin = core * (XS * YS) + lax.rem(y + YS - a, YS) * XS + lax.rem(x + XS - b, XS)
        passed.append(start(out_ref.at[origin], ZS + len(steps) + k, other))
    for copy in copies:
        copy.wait_send()
    for copy in passed:
        copy.wait()


def gather(own):
    count = ZS + 2 * XS * YS - 2
    return pl.pallas_call(
        gather_kernel,
        out_shape=jax.ShapeDtypeStruct((BLOCKS, VALUES, 128), jnp.float32),
        in_specs=[vmem()],
        out_specs=vmem(),
        scratch_shapes=[
            pltpu.VMEM((ZS, 2, 128), jnp.float32),
            pltpu.SemaphoreType.DMA((count,)),
            pltpu.SemaphoreType.DMA((count,)),
        ],
        compiler_params=params(collective_id=0, has_side_effects=True),
        cost_estimate=pl.CostEstimate(flops=10**9, bytes_accessed=2 * 10**7, transcendentals=0),
        name="gather",
    )(own)


def whole_dot(a, b, precision=None):
    return jnp.dot(a, b, precision=precision, preferred_element_type=jnp.float32)


def evaluate_kernel(g_ref, n_ref, moved_ref, kept, tiles, nodes, parts, order, weights, windows, centres, found, edges, ends, arrived, passing):
    keep = pltpu.make_async_copy(n_ref, kept, passing)
    keep.start()
    first = pl.multiple_of(lax.axis_index("inst") * 8, 8)
    nodes[...] = n_ref[:, :, pl.ds(first, 8), :] * 0.25

    for half in range(2):
        lanes = slice(half * 128, half * 128 + 128)
        rows = [
            jnp.concatenate(
                [nodes[c, p, j : j + 1, lanes] for c in range(3) for p in range(2)]
                + [jnp.zeros((2, 128), jnp.float32)],
                axis=0,
            )
            for j in range(8)
        ]
        for t, tile in enumerate(swap_blocks(rows)):
            tiles[8 * half + t] = tile
    spots = [g_ref[:, 24 + c, :] * 0.25 for c in range(3)]
    near = None
    for c in range(3):
        low = jnp.min(nodes[c]) - MARGIN
        high = jnp.max(nodes[c]) + MARGIN
        inside = (spots[c] >= low) & (spots[c] <= high)
        near = inside if near is None else near & inside
        if c == 2:
            k_low, scale = low, BINS / jnp.full((1, 1), high - low)

    def bin_of(value):
        return jnp.clip(jnp.floor((value - k_low) * scale), 0.0, BINS - 1.0)

    bins = jnp.where(near, bin_of(spots[2]), -1.0)

    bin_id = lax.broadcasted_iota(jnp.int32, (BINS, 128), 0).astype(jnp.float32)
    member = jnp.concatenate(
        [(bins[i : i + 1] == bin_id).astype(jnp.float32) for i in range(BLOCKS)], axis=0
    )
    lane = lax.broadcasted_iota(jnp.int32, (128, 256), 1)
    counting = ((lax.broadcasted_iota(jnp.int32, (128, 256), 0) <= lane) | (lane >= 128)).astype(jnp.float32)
    counts = whole_dot(member.astype(jnp.bfloat16), counting.astype(jnp.bfloat16))
    total = counts[0:BINS, 128:256]
    for i in range(1, BLOCKS):
        total = total + counts[i * BINS : (i + 1) * BINS, 128:256]
    earlier = (
        lax.broadcasted_iota(jnp.int32, (BINS, BINS), 1) < lax.broadcasted_iota(jnp.int32, (BINS, BINS), 0)
    ).astype(jnp.float32)
    running = whole_dot(earlier, total, HIGH)
    rows = []
    for i in range(BLOCKS):
        own = slice(i * BINS, (i + 1) * BINS)
        rows.append(jnp.sum(member[own] * (running + counts[own, 0:128]), axis=0, keepdims=True) - 1.0)
        running = running + counts[own, 128:256]
    position = jnp.concatenate(rows + [jnp.zeros((128 - BLOCKS, 128), jnp.float32)], axis=0).T
    for i in range(BLOCKS):
        order[i * 128 : i * 128 + 128, :] = jnp.broadcast_to(position[:, i : i + 1], (128, 128))

    k_min = jnp.min(jnp.min(nodes[2], axis=0), axis=0, keepdims=True)
    k_max = jnp.max(jnp.max(nodes[2], axis=0), axis=0, keepdims=True)
    for step in (1, 2, 4, 8):
        k_min = jnp.minimum(k_min, pltpu.roll(k_min, step, 1))
        k_max = jnp.maximum(k_max, pltpu.roll(k_max, step, 1))
    wide_id = lax.broadcasted_iota(jnp.int32, (BINS, 256), 0).astype(jnp.float32)
    wide_total = jnp.concatenate([total, total], axis=1)
    start = jnp.sum(jnp.where(wide_id < bin_of(k_min - MARGIN), wide_total, 0.0), axis=0, keepdims=True)
    stop = jnp.sum(jnp.where(wide_id <= bin_of(k_max + MARGIN), wide_total, 0.0), axis=0, keepdims=True)
    begin = jnp.floor(start * (1.0 / 32.0))
    count = jnp.floor((jnp.maximum(stop - 32.0 * begin, 1.0) + (CHUNK - 1.0)) * (1.0 / CHUNK))
    edges[0:1, :] = begin.astype(jnp.int32)
    edges[1:2, :] = count.astype(jnp.int32)
    at_tile = lax.broadcasted_iota(jnp.int32, (1, 256), 1) % 16 == 15
    beyond = jnp.max(jnp.where(at_tile, count - 1.0, 0.0), axis=1, keepdims=True)
    edges[2:3, :] = jnp.broadcast_to(beyond, (1, 256)).astype(jnp.int32)
    copy = pltpu.make_async_copy(edges, ends, arrived)
    copy.start()
    chunks = (jnp.sum(total[:, 0:1]).astype(jnp.int32) + (PLACED - 1)) // PLACED

    def split(i, carry):
        for half in range(2):
            value = g_ref[2 * i + half]
            motion = value[0:24]
            top = motion.astype(jnp.bfloat16).astype(jnp.float32)
            spot = value[24:32] * 0.25
            one = spot.astype(jnp.bfloat16).astype(jnp.float32)
            two = (spot - one).astype(jnp.bfloat16).astype(jnp.float32)
            three = spot - one - two
            parts[i, :, half * 128 : half * 128 + 128] = jnp.concatenate(
                [top, motion - top, one, two, three, jnp.zeros((8, 128), jnp.float32)], axis=0
            ).astype(jnp.bfloat16)
        return carry

    lax.fori_loop(0, BLOCKS // 2, split, 0)

    slot = lax.broadcasted_iota(jnp.int32, (1, 128), 1)

    def place_chunk(s, carry):
        sums = jnp.zeros((80, PLACED), jnp.float32)
        wanted = [(slot + (s * PLACED + 128 * half)).astype(jnp.float32) for half in range(2)]
        for i in range(BLOCKS // 2):
            at = order[i * 256 : i * 256 + 256, :]
            hit = jnp.concatenate([jnp.where(at == w, 1.0, 0.0) for w in wanted], axis=1)
            sums = sums + whole_dot(parts[i], hit.astype(jnp.bfloat16))
        short = sums[0:48]
        spot = (sums[48:56] + sums[56:64]) + sums[64:72]
        for half in range(2):
            lanes = slice(half * 128, half * 128 + 128)
            weights[2 * s + half] = short[:, lanes]
            piece = jnp.concatenate([spot[:, lanes], jnp.zeros((120, 128), jnp.float32)], axis=0).T
            at = pl.multiple_of(s * PLACED + half * 128, 128)
            for c in range(3):
                centres[c, pl.ds(at, 128), :] = jnp.broadcast_to(piece[:, c : c + 1], (128, 128))
        return carry

    lax.fori_loop(0, chunks, place_chunk, 0)

    behind = 2 * chunks
    for half in range(2):
        weights[behind + half] = jnp.zeros((48, CHUNK), jnp.float32)
        for c in range(3):
            centres[c, pl.ds(pl.multiple_of((behind + half) * CHUNK, CHUNK), CHUNK), :] = jnp.zeros((CHUNK, 128), jnp.float32)
    lane = lax.broadcasted_iota(jnp.int32, (48, CHUNK), 1)

    def shift_chunks(s, carry):
        values = [weights[2 * s + k] for k in range(3)]
        for k in range(2):
            place = 4 * (2 * s + k)
            windows[place] = values[k].astype(jnp.bfloat16)
            for r in range(1, 4):
                back = CHUNK - 32 * r
                moved = jnp.where(lane < back, pltpu.roll(values[k], back, 1), pltpu.roll(values[k + 1], back, 1))
                windows[place + r] = moved.astype(jnp.bfloat16)
        return carry

    lax.fori_loop(0, chunks, shift_chunks, 0)
    for r in range(4):
        windows[4 * behind + r] = jnp.zeros((48, CHUNK), jnp.bfloat16)

    def window(t, place):
        at = pl.multiple_of(place * 32, 32)
        spot = [centres[c, pl.ds(at, CHUNK), :] for c in range(3)]
        pieces = windows[place]
        tops, rests = [], []
        for p in range(2):
            square = None
            for c in range(3):
                gap = spot[c] - tiles[t, 2 * c + p : 2 * c + p + 1, :]
                square = gap * gap if square is None else square + gap * gap
            radius = square * lax.rsqrt(jnp.maximum(square, 1e-30))
            rest = jnp.maximum(1.0 - radius, 0.0)
            rest = rest * rest
            value = rest * rest * (4.0 * radius + 1.0)
            top = value.astype(jnp.bfloat16)
            tops.append(top)
            rests.append((value - top.astype(jnp.float32)).astype(jnp.bfloat16))
        full = whole_dot(pieces, jnp.concatenate(tops, axis=1))
        extra = whole_dot(pieces[0:32], jnp.concatenate(rests, axis=1))
        return full[0:24] + (full[24:48] + extra[0:24])

    copy.wait()

    def first_windows(group, carry):
        for k in range(GROUP):
            t = group * GROUP + k
            found[t] = window(t, ends[0, 16 * t + 15])
        return carry

    lax.fori_loop(0, 16 // GROUP, first_windows, 0)

    @pl.when(ends[2, 0] > 0)
    def _():
        def more_windows(t, carry):
            def one(k, carry):
                found[t] += window(t, ends[0, 16 * t + 15] + 4 * k)
                return carry

            return lax.fori_loop(1, ends[1, 16 * t + 15], one, carry)

        lax.fori_loop(0, 16, more_windows, 0)

    for p in range(2):
        for half in range(2):
            rows = swap_blocks([found[8 * half + t, :, p * 128 : p * 128 + 128] for t in range(8)])
            for j in range(8):
                for c in range(3):
                    into = pl.ds(c * 32 + p * 16 + half * 8 + j, 8, stride=96)
                    moved_ref[into, :] = rows[j][c * 8 : c * 8 + 8]
    keep.wait()


def evaluate(gathered, base_nodes):
    shape = jax.ShapeDtypeStruct((INST * 96, 128), jnp.float32)
    moved, kept = pl.pallas_call(
        evaluate_kernel,
        out_shape=(shape, jax.ShapeDtypeStruct(base_nodes.shape, jnp.float32)),
        in_specs=[vmem()] * 2,
        out_specs=(vmem(), vmem()),
        scratch_shapes=[
            pltpu.VMEM((16, 8, 128), jnp.float32),
            pltpu.VMEM((3, 2, 8, 256), jnp.float32),
            pltpu.VMEM((BLOCKS // 2, 80, 256), jnp.bfloat16),
            pltpu.VMEM((NC, 128), jnp.float32),
            pltpu.VMEM((NC // CHUNK + 2, 48, CHUNK), jnp.float32),
            pltpu.VMEM((4 * (NC // CHUNK + 1), 48, CHUNK), jnp.bfloat16),
            pltpu.VMEM((3, NC + 2 * CHUNK, 128), jnp.float32),
            pltpu.VMEM((16, 24, 256), jnp.float32),
            pltpu.VMEM((8, 256), jnp.int32),
            pltpu.SMEM((8, 256), jnp.int32),
            pltpu.SemaphoreType.DMA,
            pltpu.SemaphoreType.DMA,
        ],
        compiler_params=params(),
        name="evaluate",
    )(gathered, base_nodes)
    return moved.reshape(INST, 3, 2, 2, 8, 128), kept


def exchange_kernel(moved_ref, n_ref, own, halo, deformed, send, recv, send_on, recv_on):
    inst, space = lax.axis_index("inst"), lax.axis_index("space")
    behind, ahead = lax.rem(space + SPACE - 1, SPACE), lax.rem(space + 1, SPACE)
    y, core = inst // CORES, inst % CORES

    def device(a, other):
        return lax.rem(y + a, YS) * CORES + (1 - core if other else core)

    order = [(0, 1)] + [(a, other) for a in (1, YS - 1, 2) for other in (0, 1)]
    peers = [(device(*step), space) for step in order] + [(inst, behind), (inst, ahead)]
    barrier = pltpu.get_barrier_semaphore()
    for peer in peers:
        pl.semaphore_signal(barrier, inc=1, device_id=peer, device_id_type=MESH)

    def start(source, target, sent, arrived, device):
        copy = pltpu.make_async_remote_copy(
            src_ref=source,
            dst_ref=target,
            send_sem=sent,
            recv_sem=arrived,
            device_id=device,
            device_id_type=MESH,
        )
        copy.start()
        return copy

    def rows_of(strip):
        return pl.ds(pl.multiple_of(strip * 8, 8), 8)

    def add_nodes(rows):
        for c in range(3):
            for p in range(2):
                nodes = n_ref[c, p, rows, :]
                for half in range(2):
                    lanes = slice(half * 128, half * 128 + 128)
                    deformed[p, c, half, rows, :] = own[c, p, half, rows, :] + nodes[:, lanes]

    def pass_on(k, rows):
        return [
            start(
                deformed.at[side, :, :, rows, :],
                halo.at[1 - side, :, :, rows, :],
                send_on.at[side, k],
                recv_on.at[side, k],
                (inst, (behind, ahead)[side]),
            )
            for side in range(2)
        ]

    mine = rows_of(inst)
    own[:, :, :, mine, :] = moved_ref[inst]
    add_nodes(mine)
    pl.semaphore_wait(barrier, len(peers))
    copies = [
        start(moved_ref.at[peer[0]], own.at[:, :, :, mine, :], send.at[k], recv.at[k], peer)
        for k, peer in enumerate(peers[: len(order)])
    ]
    passed = pass_on(len(order), mine)
    for k, (copy, (a, other)) in enumerate(zip(copies, order)):
        copy.wait_recv()
        rows = rows_of(device(YS - a, other))
        add_nodes(rows)
        passed += pass_on(k, rows)
    for copy in copies:
        copy.wait_send()
    for copy in passed:
        copy.wait()


def exchange(moved, base_nodes):
    rows, width = base_nodes.shape[2], base_nodes.shape[3] // 2
    return pl.pallas_call(
        exchange_kernel,
        out_shape=(
            jax.ShapeDtypeStruct((3, 2, 2, rows, width), jnp.float32),
            jax.ShapeDtypeStruct((2, 3, 2, rows, width), jnp.float32),
        ),
        in_specs=[vmem(), vmem()],
        out_specs=(vmem(), vmem()),
        scratch_shapes=[
            pltpu.VMEM((2, 3, 2, rows, width), jnp.float32),
            pltpu.SemaphoreType.DMA((INST,)),
            pltpu.SemaphoreType.DMA((INST,)),
            pltpu.SemaphoreType.DMA((2, INST)),
            pltpu.SemaphoreType.DMA((2, INST)),
        ],
        compiler_params=params(collective_id=1, has_side_effects=True),
        name="exchange",
    )(moved, base_nodes)


def shifted(value, axis):
    extent = value.shape[axis]
    at = lax.broadcasted_iota(jnp.int32, value.shape, axis)
    following = pltpu.roll(value, extent - 1, axis)
    preceding = pltpu.roll(value, 1, axis)
    upper = jnp.where(at == extent - 1, 2.0 * value - preceding, following)
    lower = jnp.where(at == 0, 2.0 * value - following, preceding)
    return (upper - lower) * 0.5


def cross(a, b):
    return [
        a[1] * b[2] - a[2] * b[1],
        a[2] * b[0] - a[0] * b[2],
        a[0] * b[1] - a[1] * b[0],
    ]


def metrics_kernel(own, halo, n_ref, disp_hbm, metrics_hbm, disp, metrics, sems):
    space = lax.axis_index("space")
    copies = []

    def leave(source, target):
        copy = pltpu.make_async_copy(source, target, sems.at[len(copies)])
        copy.start()
        copies.append(copy)

    for c in range(3):
        for p in range(2):
            for half in range(2):
                disp[c, p, :, half * 128 : half * 128 + 128] = own[c, p, half]
    leave(disp, disp_hbm.at[0])

    def beside(which, c):
        return jnp.concatenate([halo[which, c, 0], halo[which, c, 1]], axis=1)

    for p in range(2):
        here = [n_ref[c, p] + disp[c, p] for c in range(3)]
        there = [n_ref[c, 1 - p] + disp[c, 1 - p] for c in range(3)]
        along_i = []
        for c in range(3):
            if p == 0:
                beyond = jnp.where(space == 0, 2.0 * here[c] - there[c], beside(0, c))
                along_i.append((there[c] - beyond) * 0.5)
            else:
                beyond = jnp.where(space == SPACE - 1, 2.0 * here[c] - there[c], beside(1, c))
                along_i.append((beyond - there[c]) * 0.5)
        along_j = [shifted(value, 0) for value in here]
        along_k = [shifted(value, 1) for value in here]
        one = cross(along_j, along_k)
        two = cross(along_k, along_i)
        three = cross(along_i, along_j)
        last = along_i[0] * one[0] + along_i[1] * one[1] + along_i[2] * one[2]
        row = 0
        for group in (one, two, three, [last]):
            for k, value in enumerate(group):
                metrics[p, row + k] = value
            rows = pl.ds(row, len(group))
            leave(metrics.at[p, rows], metrics_hbm.at[0, rows, p])
            row += len(group)
    for copy in copies:
        copy.wait()


def metric_rows(own, halo, base_nodes):
    anywhere = pl.BlockSpec(memory_space=pltpu.HBM)
    return pl.pallas_call(
        metrics_kernel,
        out_shape=(
            jax.ShapeDtypeStruct((1,) + base_nodes.shape, jnp.float32),
            jax.ShapeDtypeStruct((1, 10) + base_nodes.shape[1:], jnp.float32),
        ),
        in_specs=[vmem()] * 3,
        out_specs=(anywhere, anywhere),
        scratch_shapes=[
            pltpu.VMEM(base_nodes.shape, jnp.float32),
            pltpu.VMEM((2, 10) + base_nodes.shape[2:], jnp.float32),
            pltpu.SemaphoreType.DMA((9,)),
        ],
        compiler_params=params(),
        name="metrics",
    )(own, halo, base_nodes)


def body(amplitudes, modal_coeffs, centre_positions, base_nodes):
    modes = amplitudes.shape[1]
    own = jnp.concatenate(
        [
            modal_coeffs.transpose(1, 2, 0).reshape(3 * OWN, modes),
            amplitudes,
            jnp.pad(centre_positions, ((0, 5), (0, modes - OWN))),
        ],
        axis=0,
    )
    gathered = gather(own)
    moved, nodes = evaluate(gathered, base_nodes)
    own, halo = exchange(moved, nodes)
    return metric_rows(own, halo, nodes)


def solution(mesh):
    in_specs = (
        P(),
        P(None, None, ("inst", "space")),
        P(None, ("inst", "space")),
        P(None, "space", None, None),
    )
    out_specs = (P("inst", None, "space", None, None), P("inst", None, "space", None, None))
    return jax.shard_map(body, mesh=mesh, in_specs=in_specs, out_specs=out_specs, check_vma=False)
```

```python
import jax
import jax.numpy as jnp
from jax import lax
from jax.experimental import pallas as pl
from jax.experimental.pallas import tpu as pltpu
from jax.sharding import PartitionSpec as P

MESH = pl.DeviceIdType.MESH
HIGH = lax.Precision.HIGHEST
XS, YS, ZS, CORES = 4, 4, 16, 2
INST, SPACE = YS * CORES, XS * ZS
OWN = 8
BLOCKS = XS * YS * CORES
NC = BLOCKS * ZS * OWN
VALUES = 32
BINS = 32
CHUNK = 128
GROUP = 8
PLACED = 256
GROUPS = (NC + PLACED) // 32
MARGIN = 1.0 + 2.0**-11
VMEM_LIMIT = 32 * 1024 * 1024


def vmem():
    return pl.BlockSpec(memory_space=pltpu.VMEM)


def params(**more):
    return pltpu.CompilerParams(vmem_limit_bytes=VMEM_LIMIT, **more)


def swap_blocks(arrays):
    block = lax.broadcasted_iota(jnp.int32, arrays[0].shape, 1) // 16
    arrays = list(arrays)
    for step in (1, 2, 4):
        upper = (block & step) != 0
        for a in range(8):
            if not a & step:
                one, two = arrays[a], arrays[a | step]
                arrays[a] = jnp.where(upper, pltpu.roll(two, 16 * step, 1), one)
                arrays[a | step] = jnp.where(upper, two, pltpu.roll(one, 128 - 16 * step, 1))
    return arrays


def gather_kernel(own_ref, out_ref, zbuf, send, recv):
    inst, space = lax.axis_index("inst"), lax.axis_index("space")
    y, core = inst // CORES, inst % CORES
    x, z = space // ZS, space % ZS
    z_peers = [(inst, x * ZS + lax.rem(z + k, ZS)) for k in range(1, ZS)]
    steps = [(a, b) for a in range(YS) for b in range(XS) if a or b]
    plane_peers = [
        (lax.rem(y + a, YS) * CORES + core, lax.rem(x + b, XS) * ZS + z) for a, b in steps
    ]
    other = (y * CORES + (1 - core), space)

    def hops(a, b, c):
        return min(a, ZS - a) + min(b, YS - b) + min(c, XS - c)

    z_order = sorted(range(ZS - 1), key=lambda k: -hops(k + 1, 0, 0))
    plane_order = sorted(range(len(steps)), key=lambda k: -hops(0, *steps[k]))
    peers = [z_peers[k] for k in z_order] + [plane_peers[k] for k in plane_order] + [other]
    barrier = pltpu.get_barrier_semaphore()
    for peer in peers:
        pl.semaphore_signal(barrier, inc=1, device_id=peer, device_id_type=MESH)

    transposed = (((1,), (1,)), ((), ()))

    def high_dot(a, b):
        return lax.dot_general(a, b, transposed, precision=HIGH, preferred_element_type=jnp.float32)

    amp = own_ref[24:32]
    eye = (
        lax.broadcasted_iota(jnp.int32, (OWN, OWN), 0) == lax.broadcasted_iota(jnp.int32, (OWN, OWN), 1)
    ).astype(jnp.float32)
    own = [high_dot(own_ref[8 * c : 8 * c + 8], amp) for c in range(3)]
    own.append(high_dot(eye, own_ref[32:40, 0:OWN])[:, 0:3])
    own = jnp.concatenate(own + [jnp.zeros((OWN, 128 - 27), jnp.float32)], axis=1)
    row_id = lax.broadcasted_iota(jnp.int32, (OWN, 128), 0) % 4
    spread = jnp.zeros((OWN, 128), jnp.float32)
    for a in range(4):
        moved = own if a == 0 else pltpu.roll(own, VALUES * a, 1)
        spread = spread + jnp.where(row_id == a, moved, 0.0)
    zbuf[z] = jnp.concatenate(
        [
            jnp.sum(spread[0:4], axis=0, keepdims=True),
            jnp.sum(spread[4:8], axis=0, keepdims=True),
        ],
        axis=0,
    )

    pl.semaphore_wait(barrier, len(peers))

    def start(ref, k, peer):
        copy = pltpu.make_async_remote_copy(
            src_ref=ref,
            dst_ref=ref,
            send_sem=send.at[k],
            recv_sem=recv.at[k],
            device_id=peer,
            device_id_type=MESH,
        )
        copy.start()
        return copy

    copies = [start(zbuf.at[z], k, z_peers[k]) for k in z_order]
    for copy in reversed(copies):
        copy.wait()
    rows = jnp.concatenate([zbuf[i] for i in range(ZS)], axis=0)
    rows = jnp.concatenate([rows, jnp.zeros((128 - 2 * ZS, 128), jnp.float32)], axis=0).T
    block = rows[0:VALUES]
    for a in range(1, 4):
        block = block + pltpu.roll(rows[VALUES * a : VALUES * (a + 1)], VALUES * a, 1)
    mine = core * (XS * YS) + y * XS + x
    out_ref[mine] = block

    copies = [start(out_ref.at[mine], ZS - 1 + k, plane_peers[k]) for k in plane_order]
    passed = [start(out_ref.at[mine], ZS - 1 + len(steps), other)]
    for copy, k in reversed(list(zip(copies, plane_order))):
        copy.wait_recv()
        a, b = steps[k]
        origin = core * (XS * YS) + lax.rem(y + YS - a, YS) * XS + lax.rem(x + XS - b, XS)
        passed.append(start(out_ref.at[origin], ZS + len(steps) + k, other))
    for copy in copies:
        copy.wait_send()
    for copy in passed:
        copy.wait()


def gather(own):
    count = ZS + 2 * XS * YS - 2
    return pl.pallas_call(
        gather_kernel,
        out_shape=jax.ShapeDtypeStruct((BLOCKS, VALUES, 128), jnp.float32),
        in_specs=[vmem()],
        out_specs=vmem(),
        scratch_shapes=[
            pltpu.VMEM((ZS, 2, 128), jnp.float32),
            pltpu.SemaphoreType.DMA((count,)),
            pltpu.SemaphoreType.DMA((count,)),
        ],
        compiler_params=params(collective_id=0, has_side_effects=True),
        cost_estimate=pl.CostEstimate(flops=10**9, bytes_accessed=2 * 10**7, transcendentals=0),
        name="gather",
    )(own)


def whole_dot(a, b, precision=None):
    return jnp.dot(a, b, precision=precision, preferred_element_type=jnp.float32)


def window(tiles, centres, windows, t, place):
    spot = [
        jnp.concatenate([centres[c * GROUPS + place + k] for k in range(4)], axis=0) for c in range(3)
    ]
    pieces = windows[place]
    tops, rests = [], []
    for p in range(2):
        square = None
        for c in range(3):
            gap = spot[c] - tiles[t, 2 * c + p : 2 * c + p + 1, :]
            square = gap * gap if square is None else square + gap * gap
        radius = square * lax.rsqrt(jnp.maximum(square, 1e-30))
        rest = jnp.maximum(1.0 - radius, 0.0)
        rest = rest * rest
        value = rest * rest * (4.0 * radius + 1.0)
        top = value.astype(jnp.bfloat16)
        tops.append(top)
        rests.append((value - top.astype(jnp.float32)).astype(jnp.bfloat16))
    full = whole_dot(pieces, jnp.concatenate(tops, axis=1))
    extra = whole_dot(pieces[0:32], jnp.concatenate(rests, axis=1))
    return full[0:24] + (full[24:48] + extra[0:24])


def evaluate_kernel(g_ref, n_ref, windows, centres, tiles, found, edges, kept, nodes, parts, order, weights, ends, arrived, passing):
    keep = pltpu.make_async_copy(n_ref, kept, passing)
    keep.start()
    first = pl.multiple_of(lax.axis_index("inst") * 8, 8)
    nodes[...] = n_ref[:, :, pl.ds(first, 8), :] * 0.25

    for half in range(2):
        lanes = slice(half * 128, half * 128 + 128)
        rows = [
            jnp.concatenate(
                [nodes[c, p, j : j + 1, lanes] for c in range(3) for p in range(2)]
                + [jnp.zeros((2, 128), jnp.float32)],
                axis=0,
            )
            for j in range(8)
        ]
        for t, tile in enumerate(swap_blocks(rows)):
            tiles[8 * half + t] = tile
    spots = [g_ref[:, 24 + c, :] * 0.25 for c in range(3)]
    near = None
    for c in range(3):
        low = jnp.min(nodes[c]) - MARGIN
        high = jnp.max(nodes[c]) + MARGIN
        inside = (spots[c] >= low) & (spots[c] <= high)
        near = inside if near is None else near & inside
        if c == 2:
            k_low, scale = low, BINS / jnp.full((1, 1), high - low)

    def bin_of(value):
        return jnp.clip(jnp.floor((value - k_low) * scale), 0.0, BINS - 1.0)

    bins = jnp.where(near, bin_of(spots[2]), -1.0)

    bin_id = lax.broadcasted_iota(jnp.int32, (BINS, 128), 0).astype(jnp.float32)
    member = jnp.concatenate(
        [(bins[i : i + 1] == bin_id).astype(jnp.float32) for i in range(BLOCKS)], axis=0
    )
    lane = lax.broadcasted_iota(jnp.int32, (128, 256), 1)
    counting = ((lax.broadcasted_iota(jnp.int32, (128, 256), 0) <= lane) | (lane >= 128)).astype(jnp.float32)
    counts = whole_dot(member.astype(jnp.bfloat16), counting.astype(jnp.bfloat16))
    total = counts[0:BINS, 128:256]
    for i in range(1, BLOCKS):
        total = total + counts[i * BINS : (i + 1) * BINS, 128:256]
    earlier = (
        lax.broadcasted_iota(jnp.int32, (BINS, BINS), 1) < lax.broadcasted_iota(jnp.int32, (BINS, BINS), 0)
    ).astype(jnp.float32)
    running = whole_dot(earlier, total, HIGH)
    rows = []
    for i in range(BLOCKS):
        own = slice(i * BINS, (i + 1) * BINS)
        rows.append(jnp.sum(member[own] * (running + counts[own, 0:128]), axis=0, keepdims=True) - 1.0)
        running = running + counts[own, 128:256]
    position = jnp.concatenate(rows + [jnp.zeros((128 - BLOCKS, 128), jnp.float32)], axis=0).T
    for i in range(BLOCKS):
        order[i * 128 : i * 128 + 128, :] = jnp.broadcast_to(position[:, i : i + 1], (128, 128))

    k_min = jnp.min(jnp.min(nodes[2], axis=0), axis=0, keepdims=True)
    k_max = jnp.max(jnp.max(nodes[2], axis=0), axis=0, keepdims=True)
    for step in (1, 2, 4, 8):
        k_min = jnp.minimum(k_min, pltpu.roll(k_min, step, 1))
        k_max = jnp.maximum(k_max, pltpu.roll(k_max, step, 1))
    wide_id = lax.broadcasted_iota(jnp.int32, (BINS, 256), 0).astype(jnp.float32)
    wide_total = jnp.concatenate([total, total], axis=1)
    start = jnp.sum(jnp.where(wide_id < bin_of(k_min - MARGIN), wide_total, 0.0), axis=0, keepdims=True)
    stop = jnp.sum(jnp.where(wide_id <= bin_of(k_max + MARGIN), wide_total, 0.0), axis=0, keepdims=True)
    begin = jnp.floor(start * (1.0 / 32.0))
    count = jnp.floor((jnp.maximum(stop - 32.0 * begin, 1.0) + (CHUNK - 1.0)) * (1.0 / CHUNK))
    edges[0:1, :] = begin.astype(jnp.int32)
    edges[1:2, :] = count.astype(jnp.int32)
    at_tile = lax.broadcasted_iota(jnp.int32, (1, 256), 1) % 16 == 15
    beyond = jnp.max(jnp.where(at_tile, count - 1.0, 0.0), axis=1, keepdims=True)
    edges[2:3, :] = jnp.broadcast_to(beyond, (1, 256)).astype(jnp.int32)
    copy = pltpu.make_async_copy(edges, ends, arrived)
    copy.start()
    chunks = (jnp.sum(total[:, 0:1]).astype(jnp.int32) + (PLACED - 1)) // PLACED

    def split(i, carry):
        for half in range(2):
            value = g_ref[2 * i + half]
            motion = value[0:24]
            top = motion.astype(jnp.bfloat16).astype(jnp.float32)
            spot = value[24:32] * 0.25
            one = spot.astype(jnp.bfloat16).astype(jnp.float32)
            two = (spot - one).astype(jnp.bfloat16).astype(jnp.float32)
            three = spot - one - two
            parts[i, :, half * 128 : half * 128 + 128] = jnp.concatenate(
                [top, motion - top, one, two, three, jnp.zeros((8, 128), jnp.float32)], axis=0
            ).astype(jnp.bfloat16)
        return carry

    lax.fori_loop(0, BLOCKS // 2, split, 0)

    slot = lax.broadcasted_iota(jnp.int32, (1, 128), 1)

    def place_chunk(s, carry):
        sums = jnp.zeros((80, PLACED), jnp.float32)
        wanted = [(slot + (s * PLACED + 128 * half)).astype(jnp.float32) for half in range(2)]
        for i in range(BLOCKS // 2):
            at = order[i * 256 : i * 256 + 256, :]
            hit = jnp.concatenate([jnp.where(at == w, 1.0, 0.0) for w in wanted], axis=1)
            sums = sums + whole_dot(parts[i], hit.astype(jnp.bfloat16))
        short = sums[0:48]
        spot = (sums[48:56] + sums[56:64]) + sums[64:72]
        for half in range(2):
            lanes = slice(half * 128, half * 128 + 128)
            weights[2 * s + half] = short[:, lanes]
            piece = jnp.concatenate([spot[:, lanes], jnp.zeros((120, 128), jnp.float32)], axis=0).T
            for c in range(3):
                into = pl.ds(c * GROUPS + s * 8 + half * 4, 4)
                centres[into] = jnp.broadcast_to(piece[:, c : c + 1], (128, 128)).reshape(4, 32, 128)
        return carry

    lax.fori_loop(0, chunks, place_chunk, 0)

    behind = 2 * chunks
    for half in range(2):
        weights[behind + half] = jnp.zeros((48, CHUNK), jnp.float32)
        for c in range(3):
            centres[pl.ds(c * GROUPS + 4 * (behind + half), 4)] = jnp.zeros((4, 32, 128), jnp.float32)
    lane = lax.broadcasted_iota(jnp.int32, (48, CHUNK), 1)

    def shift_chunks(s, carry):
        values = [weights[2 * s + k] for k in range(3)]
        for k in range(2):
            place = 4 * (2 * s + k)
            windows[place] = values[k].astype(jnp.bfloat16)
            for r in range(1, 4):
                back = CHUNK - 32 * r
                moved = jnp.where(lane < back, pltpu.roll(values[k], back, 1), pltpu.roll(values[k + 1], back, 1))
                windows[place + r] = moved.astype(jnp.bfloat16)
        return carry

    lax.fori_loop(0, chunks, shift_chunks, 0)
    for r in range(4):
        windows[4 * behind + r] = jnp.zeros((48, CHUNK), jnp.bfloat16)

    found[...] = jnp.zeros_like(found)
    copy.wait()

    @pl.when(ends[2, 0] > 0)
    def _():
        def more_windows(t, carry):
            def one(k, carry):
                found[t] += window(tiles, centres, windows, t, ends[0, 16 * t + 15] + 4 * k)
                return carry

            return lax.fori_loop(1, ends[1, 16 * t + 15], one, carry)

        lax.fori_loop(0, 16, more_windows, 0)

    keep.wait()


def evaluate(gathered, base_nodes):
    shape = jax.ShapeDtypeStruct
    return pl.pallas_call(
        evaluate_kernel,
        out_shape=(
            shape((4 * (NC // CHUNK + 1), 48, CHUNK), jnp.bfloat16),
            shape((3 * GROUPS, 32, 128), jnp.float32),
            shape((16, 8, 128), jnp.float32),
            shape((16, 24, 256), jnp.float32),
            shape((8, 256), jnp.int32),
            shape(base_nodes.shape, jnp.float32),
        ),
        in_specs=[vmem()] * 2,
        out_specs=(vmem(),) * 6,
        scratch_shapes=[
            pltpu.VMEM((3, 2, 8, 256), jnp.float32),
            pltpu.VMEM((BLOCKS // 2, 80, 256), jnp.bfloat16),
            pltpu.VMEM((NC, 128), jnp.float32),
            pltpu.VMEM((NC // CHUNK + 2, 48, CHUNK), jnp.float32),
            pltpu.SMEM((8, 256), jnp.int32),
            pltpu.SemaphoreType.DMA,
            pltpu.SemaphoreType.DMA,
        ],
        compiler_params=params(),
        name="evaluate",
    )(gathered, base_nodes)


def exchange_kernel(windows, centres, tiles, more, edges, n_ref, own, halo, found, moved, deformed, send, recv, send_on, recv_on):
    inst, space = lax.axis_index("inst"), lax.axis_index("space")
    behind, ahead = lax.rem(space + SPACE - 1, SPACE), lax.rem(space + 1, SPACE)
    y, core = inst // CORES, inst % CORES

    def device(a, other):
        return lax.rem(y + a, YS) * CORES + (1 - core if other else core)

    order = [(0, 1)] + [(a, other) for a in (1, YS - 1, 2) for other in (0, 1)]
    peers = [(device(*step), space) for step in order] + [(inst, behind), (inst, ahead)]
    barrier = pltpu.get_barrier_semaphore()
    for peer in peers:
        pl.semaphore_signal(barrier, inc=1, device_id=peer, device_id_type=MESH)

    def start(source, target, sent, arrived, device):
        copy = pltpu.make_async_remote_copy(
            src_ref=source,
            dst_ref=target,
            send_sem=sent,
            recv_sem=arrived,
            device_id=device,
            device_id_type=MESH,
        )
        copy.start()
        return copy

    def first_windows(group, carry):
        for k in range(GROUP):
            t = group * GROUP + k
            found[t] = more[t] + window(tiles, centres, windows, t, edges[0, 16 * t + 15])
        return carry

    lax.fori_loop(0, 16 // GROUP, first_windows, 0)
    for p in range(2):
        for half in range(2):
            rows = swap_blocks([found[8 * half + t, :, p * 128 : p * 128 + 128] for t in range(8)])
            for j in range(8):
                for c in range(3):
                    into = pl.ds(c * 32 + p * 16 + half * 8 + j, 8, stride=96)
                    moved[into, :] = rows[j][c * 8 : c * 8 + 8]

    def add_nodes(strip):
        rows = pl.ds(pl.multiple_of(strip * 8, 8), 8)
        for c in range(3):
            for p in range(2):
                nodes = n_ref[c, p, rows, :]
                for half in range(2):
                    at, to = c * 32 + p * 16 + half * 8, c * 16 + half * 8
                    lanes = slice(half * 128, half * 128 + 128)
                    deformed[p, strip, to : to + 8, :] = own[strip, at : at + 8, :] + nodes[:, lanes]

    def pass_on(k, strip):
        return [
            start(
                deformed.at[side, strip],
                halo.at[1 - side, strip],
                send_on.at[side, k],
                recv_on.at[side, k],
                (inst, (behind, ahead)[side]),
            )
            for side in range(2)
        ]

    def rows_for(target):
        return pl.ds(pl.multiple_of(target * 96, 96), 96)

    own[inst] = moved[rows_for(inst), :]
    add_nodes(inst)
    pl.semaphore_wait(barrier, len(peers))
    copies = [
        start(moved.at[rows_for(peer[0])], own.at[inst], send.at[k], recv.at[k], peer)
        for k, peer in enumerate(peers[: len(order)])
    ]
    passed = pass_on(len(order), inst)
    for k, (copy, (a, other)) in enumerate(zip(copies, order)):
        copy.wait_recv()
        strip = device(YS - a, other)
        add_nodes(strip)
        passed += pass_on(k, strip)
    for copy in copies:
        copy.wait_send()
    for copy in passed:
        copy.wait()


def exchange(*arrays):
    return pl.pallas_call(
        exchange_kernel,
        out_shape=(
            jax.ShapeDtypeStruct((INST, 96, 128), jnp.float32),
            jax.ShapeDtypeStruct((2, INST, 48, 128), jnp.float32),
        ),
        in_specs=[vmem()] * 4 + [pl.BlockSpec(memory_space=pltpu.SMEM), vmem()],
        out_specs=(vmem(), vmem()),
        scratch_shapes=[
            pltpu.VMEM((16, 24, 256), jnp.float32),
            pltpu.VMEM((INST * 96, 128), jnp.float32),
            pltpu.VMEM((2, INST, 48, 128), jnp.float32),
            pltpu.SemaphoreType.DMA((INST,)),
            pltpu.SemaphoreType.DMA((INST,)),
            pltpu.SemaphoreType.DMA((2, INST)),
            pltpu.SemaphoreType.DMA((2, INST)),
        ],
        compiler_params=params(collective_id=1, has_side_effects=True),
        name="exchange",
    )(*arrays)


def shifted(value, axis):
    extent = value.shape[axis]
    at = lax.broadcasted_iota(jnp.int32, value.shape, axis)
    following = pltpu.roll(value, extent - 1, axis)
    preceding = pltpu.roll(value, 1, axis)
    upper = jnp.where(at == extent - 1, 2.0 * value - preceding, following)
    lower = jnp.where(at == 0, 2.0 * value - following, preceding)
    return (upper - lower) * 0.5


def cross(a, b):
    return [
        a[1] * b[2] - a[2] * b[1],
        a[2] * b[0] - a[0] * b[2],
        a[0] * b[1] - a[1] * b[0],
    ]


def metrics_kernel(own, halo, n_ref, disp_hbm, metrics_hbm, disp, ends, metrics, sems):
    space = lax.axis_index("space")
    copies = []

    def leave(source, target):
        copy = pltpu.make_async_copy(source, target, sems.at[len(copies)])
        copy.start()
        copies.append(copy)

    def strip_rows(strip, carry):
        rows = pl.ds(pl.multiple_of(strip * 8, 8), 8)
        for c in range(3):
            for half in range(2):
                lanes = slice(half * 128, half * 128 + 128)
                for p in range(2):
                    at = c * 32 + p * 16 + half * 8
                    disp[c, p, rows, lanes] = own[strip, at : at + 8, :]
                    at = c * 16 + half * 8
                    ends[p, c, rows, lanes] = halo[p, strip, at : at + 8, :]
        return carry

    lax.fori_loop(0, INST, strip_rows, 0, unroll=True)
    leave(disp, disp_hbm.at[0])

    for p in range(2):
        here = [n_ref[c, p] + disp[c, p] for c in range(3)]
        there = [n_ref[c, 1 - p] + disp[c, 1 - p] for c in range(3)]
        along_i = []
        for c in range(3):
            if p == 0:
                beyond = jnp.where(space == 0, 2.0 * here[c] - there[c], ends[0, c])
                along_i.append((there[c] - beyond) * 0.5)
            else:
                beyond = jnp.where(space == SPACE - 1, 2.0 * here[c] - there[c], ends[1, c])
                along_i.append((beyond - there[c]) * 0.5)
        along_j = [shifted(value, 0) for value in here]
        along_k = [shifted(value, 1) for value in here]
        one = cross(along_j, along_k)
        two = cross(along_k, along_i)
        three = cross(along_i, along_j)
        last = along_i[0] * one[0] + along_i[1] * one[1] + along_i[2] * one[2]
        row = 0
        for group in (one, two, three, [last]):
            for k, value in enumerate(group):
                metrics[p, row + k] = value
            rows = pl.ds(row, len(group))
            leave(metrics.at[p, rows], metrics_hbm.at[0, rows, p])
            row += len(group)
    for copy in copies:
        copy.wait()


def metric_rows(own, halo, base_nodes):
    anywhere = pl.BlockSpec(memory_space=pltpu.HBM)
    return pl.pallas_call(
        metrics_kernel,
        out_shape=(
            jax.ShapeDtypeStruct((1,) + base_nodes.shape, jnp.float32),
            jax.ShapeDtypeStruct((1, 10) + base_nodes.shape[1:], jnp.float32),
        ),
        in_specs=[vmem()] * 3,
        out_specs=(anywhere, anywhere),
        scratch_shapes=[
            pltpu.VMEM(base_nodes.shape, jnp.float32),
            pltpu.VMEM((2, 3) + base_nodes.shape[2:], jnp.float32),
            pltpu.VMEM((2, 10) + base_nodes.shape[2:], jnp.float32),
            pltpu.SemaphoreType.DMA((9,)),
        ],
        compiler_params=params(),
        name="metrics",
    )(own, halo, base_nodes)


def body(amplitudes, modal_coeffs, centre_positions, base_nodes):
    modes = amplitudes.shape[1]
    own = jnp.concatenate(
        [
            modal_coeffs.transpose(1, 2, 0).reshape(3 * OWN, modes),
            amplitudes,
            jnp.pad(centre_positions, ((0, 5), (0, modes - OWN))),
        ],
        axis=0,
    )
    gathered = gather(own)
    *placed, nodes = evaluate(gathered, base_nodes)
    own, halo = exchange(*placed, nodes)
    return metric_rows(own, halo, nodes)


def solution(mesh):
    in_specs = (
        P(),
        P(None, None, ("inst", "space")),
        P(None, ("inst", "space")),
        P(None, "space", None, None),
    )
    out_specs = (P("inst", None, "space", None, None), P("inst", None, "space", None, None))
    return jax.shard_map(body, mesh=mesh, in_specs=in_specs, out_specs=out_specs, check_vma=False)
```

```python
import jax
import jax.numpy as jnp
from jax import lax
from jax.experimental import pallas as pl
from jax.experimental.pallas import tpu as pltpu
from jax.sharding import PartitionSpec as P

MESH = pl.DeviceIdType.MESH
HIGH = lax.Precision.HIGHEST
XS, YS, ZS, CORES = 4, 4, 16, 2
INST, SPACE = YS * CORES, XS * ZS
OWN = 8
BLOCKS = XS * YS * CORES
NC = BLOCKS * ZS * OWN
VALUES = 32
BINS = 32
CHUNK = 128
GROUP = 8
PLACED = 256
GROUPS = (NC + PLACED) // 32
MARGIN = 1.0 + 2.0**-11
VMEM_LIMIT = 32 * 1024 * 1024


def vmem():
    return pl.BlockSpec(memory_space=pltpu.VMEM)


def params(**more):
    return pltpu.CompilerParams(vmem_limit_bytes=VMEM_LIMIT, **more)


def swap_blocks(arrays):
    block = lax.broadcasted_iota(jnp.int32, arrays[0].shape, 1) // 16
    arrays = list(arrays)
    for step in (1, 2, 4):
        upper = (block & step) != 0
        for a in range(8):
            if not a & step:
                one, two = arrays[a], arrays[a | step]
                arrays[a] = jnp.where(upper, pltpu.roll(two, 16 * step, 1), one)
                arrays[a | step] = jnp.where(upper, two, pltpu.roll(one, 128 - 16 * step, 1))
    return arrays


def gather_kernel(own_ref, out_ref, zbuf, send, recv):
    inst, space = lax.axis_index("inst"), lax.axis_index("space")
    y, core = inst // CORES, inst % CORES
    x, z = space // ZS, space % ZS
    z_peers = [(inst, x * ZS + lax.rem(z + k, ZS)) for k in range(1, ZS)]
    steps = [(a, b) for a in range(YS) for b in range(XS) if a or b]
    plane_peers = [
        (lax.rem(y + a, YS) * CORES + core, lax.rem(x + b, XS) * ZS + z) for a, b in steps
    ]
    other = (y * CORES + (1 - core), space)

    def hops(a, b, c):
        return min(a, ZS - a) + min(b, YS - b) + min(c, XS - c)

    z_order = sorted(range(ZS - 1), key=lambda k: -hops(k + 1, 0, 0))
    plane_order = sorted(range(len(steps)), key=lambda k: -hops(0, *steps[k]))
    peers = [z_peers[k] for k in z_order] + [plane_peers[k] for k in plane_order] + [other]
    barrier = pltpu.get_barrier_semaphore()
    for peer in peers:
        pl.semaphore_signal(barrier, inc=1, device_id=peer, device_id_type=MESH)

    transposed = (((1,), (1,)), ((), ()))

    def high_dot(a, b):
        return lax.dot_general(a, b, transposed, precision=HIGH, preferred_element_type=jnp.float32)

    amp = own_ref[24:32]
    eye = (
        lax.broadcasted_iota(jnp.int32, (OWN, OWN), 0) == lax.broadcasted_iota(jnp.int32, (OWN, OWN), 1)
    ).astype(jnp.float32)
    own = [high_dot(own_ref[8 * c : 8 * c + 8], amp) for c in range(3)]
    own.append(high_dot(eye, own_ref[32:40, 0:OWN])[:, 0:3])
    own = jnp.concatenate(own + [jnp.zeros((OWN, 128 - 27), jnp.float32)], axis=1)
    row_id = lax.broadcasted_iota(jnp.int32, (OWN, 128), 0) % 4
    spread = jnp.zeros((OWN, 128), jnp.float32)
    for a in range(4):
        moved = own if a == 0 else pltpu.roll(own, VALUES * a, 1)
        spread = spread + jnp.where(row_id == a, moved, 0.0)
    zbuf[z] = jnp.concatenate(
        [
            jnp.sum(spread[0:4], axis=0, keepdims=True),
            jnp.sum(spread[4:8], axis=0, keepdims=True),
        ],
        axis=0,
    )

    pl.semaphore_wait(barrier, len(peers))

    def start(ref, k, peer):
        copy = pltpu.make_async_remote_copy(
            src_ref=ref,
            dst_ref=ref,
            send_sem=send.at[k],
            recv_sem=recv.at[k],
            device_id=peer,
            device_id_type=MESH,
        )
        copy.start()
        return copy

    copies = [start(zbuf.at[z], k, z_peers[k]) for k in z_order]
    for copy in reversed(copies):
        copy.wait()
    rows = jnp.concatenate([zbuf[i] for i in range(ZS)], axis=0)
    rows = jnp.concatenate([rows, jnp.zeros((128 - 2 * ZS, 128), jnp.float32)], axis=0).T
    block = rows[0:VALUES]
    for a in range(1, 4):
        block = block + pltpu.roll(rows[VALUES * a : VALUES * (a + 1)], VALUES * a, 1)
    mine = core * (XS * YS) + y * XS + x
    out_ref[mine] = block

    copies = [start(out_ref.at[mine], ZS - 1 + k, plane_peers[k]) for k in plane_order]
    passed = [start(out_ref.at[mine], ZS - 1 + len(steps), other)]
    for copy, k in reversed(list(zip(copies, plane_order))):
        copy.wait_recv()
        a, b = steps[k]
        origin = core * (XS * YS) + lax.rem(y + YS - a, YS) * XS + lax.rem(x + XS - b, XS)
        passed.append(start(out_ref.at[origin], ZS + len(steps) + k, other))
    for copy in copies:
        copy.wait_send()
    for copy in passed:
        copy.wait()


def gather(own):
    count = ZS + 2 * XS * YS - 2
    return pl.pallas_call(
        gather_kernel,
        out_shape=jax.ShapeDtypeStruct((BLOCKS, VALUES, 128), jnp.float32),
        in_specs=[vmem()],
        out_specs=vmem(),
        scratch_shapes=[
            pltpu.VMEM((ZS, 2, 128), jnp.float32),
            pltpu.SemaphoreType.DMA((count,)),
            pltpu.SemaphoreType.DMA((count,)),
        ],
        compiler_params=params(collective_id=0, has_side_effects=True),
        cost_estimate=pl.CostEstimate(flops=10**9, bytes_accessed=2 * 10**7, transcendentals=0),
        name="gather",
    )(own)


def whole_dot(a, b, precision=None):
    return jnp.dot(a, b, precision=precision, preferred_element_type=jnp.float32)


def window(tiles, centres, windows, t, place):
    spot = [
        jnp.concatenate([centres[c * GROUPS + place + k] for k in range(4)], axis=0) for c in range(3)
    ]
    pieces = windows[place]
    tops, rests = [], []
    for p in range(2):
        square = None
        for c in range(3):
            gap = spot[c] - tiles[t, 2 * c + p : 2 * c + p + 1, :]
            square = gap * gap if square is None else square + gap * gap
        radius = square * lax.rsqrt(jnp.maximum(square, 1e-30))
        rest = jnp.maximum(1.0 - radius, 0.0)
        rest = rest * rest
        value = rest * rest * (4.0 * radius + 1.0)
        top = value.astype(jnp.bfloat16)
        tops.append(top)
        rests.append((value - top.astype(jnp.float32)).astype(jnp.bfloat16))
    full = whole_dot(pieces, jnp.concatenate(tops, axis=1))
    extra = whole_dot(pieces[0:32], jnp.concatenate(rests, axis=1))
    return full[0:24] + (full[24:48] + extra[0:24])


def evaluate_kernel(g_ref, n_ref, windows, centres, tiles, found, edges, kept, nodes, parts, order, weights, ends, arrived, passing):
    keep = pltpu.make_async_copy(n_ref, kept, passing)
    keep.start()
    first = pl.multiple_of(lax.axis_index("inst") * 8, 8)
    nodes[...] = n_ref[:, :, pl.ds(first, 8), :] * 0.25

    for half in range(2):
        lanes = slice(half * 128, half * 128 + 128)
        rows = [
            jnp.concatenate(
                [nodes[c, p, j : j + 1, lanes] for c in range(3) for p in range(2)]
                + [jnp.zeros((2, 128), jnp.float32)],
                axis=0,
            )
            for j in range(8)
        ]
        for t, tile in enumerate(swap_blocks(rows)):
            tiles[8 * half + t] = tile
    spots = [g_ref[:, 24 + c, :] * 0.25 for c in range(3)]
    near = None
    for c in range(3):
        low = jnp.min(nodes[c]) - MARGIN
        high = jnp.max(nodes[c]) + MARGIN
        inside = (spots[c] >= low) & (spots[c] <= high)
        near = inside if near is None else near & inside
        if c == 2:
            k_low, scale = low, BINS / jnp.full((1, 1), high - low)

    def bin_of(value):
        return jnp.clip(jnp.floor((value - k_low) * scale), 0.0, BINS - 1.0)

    bins = jnp.where(near, bin_of(spots[2]), -1.0)

    bin_id = lax.broadcasted_iota(jnp.int32, (BINS, 128), 0).astype(jnp.float32)
    member = jnp.concatenate(
        [(bins[i : i + 1] == bin_id).astype(jnp.float32) for i in range(BLOCKS)], axis=0
    )
    lane = lax.broadcasted_iota(jnp.int32, (128, 256), 1)
    counting = ((lax.broadcasted_iota(jnp.int32, (128, 256), 0) <= lane) | (lane >= 128)).astype(jnp.float32)
    counts = whole_dot(member.astype(jnp.bfloat16), counting.astype(jnp.bfloat16))
    total = counts[0:BINS, 128:256]
    for i in range(1, BLOCKS):
        total = total + counts[i * BINS : (i + 1) * BINS, 128:256]
    earlier = (
        lax.broadcasted_iota(jnp.int32, (BINS, BINS), 1) < lax.broadcasted_iota(jnp.int32, (BINS, BINS), 0)
    ).astype(jnp.float32)
    running = whole_dot(earlier, total, HIGH)
    rows = []
    for i in range(BLOCKS):
        own = slice(i * BINS, (i + 1) * BINS)
        rows.append(jnp.sum(member[own] * (running + counts[own, 0:128]), axis=0, keepdims=True) - 1.0)
        running = running + counts[own, 128:256]
    position = jnp.concatenate(rows + [jnp.zeros((128 - BLOCKS, 128), jnp.float32)], axis=0).T
    for i in range(BLOCKS):
        order[i * 128 : i * 128 + 128, :] = jnp.broadcast_to(position[:, i : i + 1], (128, 128))

    k_min = jnp.min(jnp.min(nodes[2], axis=0), axis=0, keepdims=True)
    k_max = jnp.max(jnp.max(nodes[2], axis=0), axis=0, keepdims=True)
    for step in (1, 2, 4, 8):
        k_min = jnp.minimum(k_min, pltpu.roll(k_min, step, 1))
        k_max = jnp.maximum(k_max, pltpu.roll(k_max, step, 1))
    wide_id = lax.broadcasted_iota(jnp.int32, (BINS, 256), 0).astype(jnp.float32)
    wide_total = jnp.concatenate([total, total], axis=1)
    start = jnp.sum(jnp.where(wide_id < bin_of(k_min - MARGIN), wide_total, 0.0), axis=0, keepdims=True)
    stop = jnp.sum(jnp.where(wide_id <= bin_of(k_max + MARGIN), wide_total, 0.0), axis=0, keepdims=True)
    begin = jnp.floor(start * (1.0 / 32.0))
    count = jnp.floor((jnp.maximum(stop - 32.0 * begin, 1.0) + (CHUNK - 1.0)) * (1.0 / CHUNK))
    edges[0:1, :] = begin.astype(jnp.int32)
    edges[1:2, :] = count.astype(jnp.int32)
    at_tile = lax.broadcasted_iota(jnp.int32, (1, 256), 1) % 16 == 15
    more = at_tile & (count > 1.0)
    tile_id = lax.broadcasted_iota(jnp.int32, (1, 256), 1) // 16
    lowest = jnp.min(jnp.where(more, tile_id, 16), axis=1, keepdims=True)
    highest = jnp.max(jnp.where(more, tile_id + 1, 0), axis=1, keepdims=True)
    edges[2:3, :] = jnp.broadcast_to(lowest, (1, 256))
    edges[3:4, :] = jnp.broadcast_to(highest, (1, 256))
    copy = pltpu.make_async_copy(edges, ends, arrived)
    copy.start()
    chunks = (jnp.sum(total[:, 0:1]).astype(jnp.int32) + (PLACED - 1)) // PLACED

    def split(i, carry):
        for half in range(2):
            value = g_ref[2 * i + half]
            motion = value[0:24]
            top = motion.astype(jnp.bfloat16).astype(jnp.float32)
            spot = value[24:32] * 0.25
            one = spot.astype(jnp.bfloat16).astype(jnp.float32)
            two = (spot - one).astype(jnp.bfloat16).astype(jnp.float32)
            three = spot - one - two
            parts[i, :, half * 128 : half * 128 + 128] = jnp.concatenate(
                [top, motion - top, one, two, three, jnp.zeros((8, 128), jnp.float32)], axis=0
            ).astype(jnp.bfloat16)
        return carry

    lax.fori_loop(0, BLOCKS // 2, split, 0)

    slot = lax.broadcasted_iota(jnp.int32, (1, 128), 1)

    def place_chunk(s, carry):
        sums = jnp.zeros((80, PLACED), jnp.float32)
        wanted = [(slot + (s * PLACED + 128 * half)).astype(jnp.float32) for half in range(2)]
        for i in range(BLOCKS // 2):
            at = order[i * 256 : i * 256 + 256, :]
            hit = jnp.concatenate([jnp.where(at == w, 1.0, 0.0) for w in wanted], axis=1)
            sums = sums + whole_dot(parts[i], hit.astype(jnp.bfloat16))
        short = sums[0:48]
        spot = (sums[48:56] + sums[56:64]) + sums[64:72]
        for half in range(2):
            lanes = slice(half * 128, half * 128 + 128)
            weights[2 * s + half] = short[:, lanes]
            piece = jnp.concatenate([spot[:, lanes], jnp.zeros((120, 128), jnp.float32)], axis=0).T
            for c in range(3):
                into = pl.ds(c * GROUPS + s * 8 + half * 4, 4)
                centres[into] = jnp.broadcast_to(piece[:, c : c + 1], (128, 128)).reshape(4, 32, 128)
        return carry

    lax.fori_loop(0, chunks, place_chunk, 0)

    behind = 2 * chunks
    for half in range(2):
        weights[behind + half] = jnp.zeros((48, CHUNK), jnp.float32)
        for c in range(3):
            centres[pl.ds(c * GROUPS + 4 * (behind + half), 4)] = jnp.zeros((4, 32, 128), jnp.float32)
    lane = lax.broadcasted_iota(jnp.int32, (48, CHUNK), 1)

    def shift_chunks(s, carry):
        values = [weights[2 * s + k] for k in range(3)]
        for k in range(2):
            place = 4 * (2 * s + k)
            windows[place] = values[k].astype(jnp.bfloat16)
            for r in range(1, 4):
                back = CHUNK - 32 * r
                moved = jnp.where(lane < back, pltpu.roll(values[k], back, 1), pltpu.roll(values[k + 1], back, 1))
                windows[place + r] = moved.astype(jnp.bfloat16)
        return carry

    lax.fori_loop(0, chunks, shift_chunks, 0)
    for r in range(4):
        windows[4 * behind + r] = jnp.zeros((48, CHUNK), jnp.bfloat16)

    found[...] = jnp.zeros_like(found)
    copy.wait()

    def more_windows(t, carry):
        def one(k, carry):
            found[t] += window(tiles, centres, windows, t, ends[0, 16 * t + 15] + 4 * k)
            return carry

        return lax.fori_loop(1, ends[1, 16 * t + 15], one, carry)

    lax.fori_loop(ends[2, 0], ends[3, 0], more_windows, 0)
    keep.wait()


def evaluate(gathered, base_nodes):
    shape = jax.ShapeDtypeStruct
    return pl.pallas_call(
        evaluate_kernel,
        out_shape=(
            shape((4 * (NC // CHUNK + 1), 48, CHUNK), jnp.bfloat16),
            shape((3 * GROUPS, 32, 128), jnp.float32),
            shape((16, 8, 128), jnp.float32),
            shape((16, 24, 256), jnp.float32),
            shape((8, 256), jnp.int32),
            shape(base_nodes.shape, jnp.float32),
        ),
        in_specs=[vmem()] * 2,
        out_specs=(vmem(),) * 6,
        scratch_shapes=[
            pltpu.VMEM((3, 2, 8, 256), jnp.float32),
            pltpu.VMEM((BLOCKS // 2, 80, 256), jnp.bfloat16),
            pltpu.VMEM((NC, 128), jnp.float32),
            pltpu.VMEM((NC // CHUNK + 2, 48, CHUNK), jnp.float32),
            pltpu.SMEM((8, 256), jnp.int32),
            pltpu.SemaphoreType.DMA,
            pltpu.SemaphoreType.DMA,
        ],
        compiler_params=params(),
        name="evaluate",
    )(gathered, base_nodes)


def exchange_kernel(windows, centres, tiles, more, edges, n_ref, own, halo, found, moved, deformed, send, recv, send_on, recv_on):
    inst, space = lax.axis_index("inst"), lax.axis_index("space")
    behind, ahead = lax.rem(space + SPACE - 1, SPACE), lax.rem(space + 1, SPACE)
    y, core = inst // CORES, inst % CORES

    def device(a, other):
        return lax.rem(y + a, YS) * CORES + (1 - core if other else core)

    order = [(0, 1)] + [(a, other) for a in (1, YS - 1, 2) for other in (0, 1)]
    peers = [(device(*step), space) for step in order] + [(inst, behind), (inst, ahead)]
    barrier = pltpu.get_barrier_semaphore()
    for peer in peers:
        pl.semaphore_signal(barrier, inc=1, device_id=peer, device_id_type=MESH)

    def start(source, target, sent, arrived, device):
        copy = pltpu.make_async_remote_copy(
            src_ref=source,
            dst_ref=target,
            send_sem=sent,
            recv_sem=arrived,
            device_id=device,
            device_id_type=MESH,
        )
        copy.start()
        return copy

    def first_windows(group, carry):
        for k in range(GROUP):
            t = group * GROUP + k
            found[t] = more[t] + window(tiles, centres, windows, t, edges[0, 16 * t + 15])
        return carry

    lax.fori_loop(0, 16 // GROUP, first_windows, 0)
    for p in range(2):
        for half in range(2):
            rows = swap_blocks([found[8 * half + t, :, p * 128 : p * 128 + 128] for t in range(8)])
            for j in range(8):
                for c in range(3):
                    into = pl.ds(c * 32 + p * 16 + half * 8 + j, 8, stride=96)
                    moved[into, :] = rows[j][c * 8 : c * 8 + 8]

    def add_nodes(strip):
        rows = pl.ds(pl.multiple_of(strip * 8, 8), 8)
        for c in range(3):
            for p in range(2):
                nodes = n_ref[c, p, rows, :]
                for half in range(2):
                    at, to = c * 32 + p * 16 + half * 8, c * 16 + half * 8
                    lanes = slice(half * 128, half * 128 + 128)
                    deformed[p, strip, to : to + 8, :] = own[strip, at : at + 8, :] + nodes[:, lanes]

    def pass_on(k, chip):
        strips = pl.ds(CORES * chip, CORES)
        return [
            start(
                deformed.at[side, strips],
                halo.at[1 - side, strips],
                send_on.at[side, k],
                recv_on.at[side, k],
                (inst, (behind, ahead)[side]),
            )
            for side in range(2)
        ]

    def rows_for(target):
        return pl.ds(pl.multiple_of(target * 96, 96), 96)

    own[inst] = moved[rows_for(inst), :]
    add_nodes(inst)
    pl.semaphore_wait(barrier, len(peers))
    copies = [
        start(moved.at[rows_for(peer[0])], own.at[inst], send.at[k], recv.at[k], peer)
        for k, peer in enumerate(peers[: len(order)])
    ]
    passed = []
    for k, a in enumerate((0, 1, YS - 1, 2)):
        for copy, step in zip(copies, order):
            if step[0] == a:
                copy.wait_recv()
                add_nodes(device(YS - a, step[1]))
        passed += pass_on(k, lax.rem(y + YS - a, YS))
    for copy in copies:
        copy.wait_send()
    for copy in passed:
        copy.wait()


def exchange(*arrays):
    return pl.pallas_call(
        exchange_kernel,
        out_shape=(
            jax.ShapeDtypeStruct((INST, 96, 128), jnp.float32),
            jax.ShapeDtypeStruct((2, INST, 48, 128), jnp.float32),
        ),
        in_specs=[vmem()] * 4 + [pl.BlockSpec(memory_space=pltpu.SMEM), vmem()],
        out_specs=(vmem(), vmem()),
        scratch_shapes=[
            pltpu.VMEM((16, 24, 256), jnp.float32),
            pltpu.VMEM((INST * 96, 128), jnp.float32),
            pltpu.VMEM((2, INST, 48, 128), jnp.float32),
            pltpu.SemaphoreType.DMA((INST,)),
            pltpu.SemaphoreType.DMA((INST,)),
            pltpu.SemaphoreType.DMA((2, YS)),
            pltpu.SemaphoreType.DMA((2, YS)),
        ],
        compiler_params=params(collective_id=1, has_side_effects=True),
        name="exchange",
    )(*arrays)


def shifted(value, axis):
    extent = value.shape[axis]
    at = lax.broadcasted_iota(jnp.int32, value.shape, axis)
    following = pltpu.roll(value, extent - 1, axis)
    preceding = pltpu.roll(value, 1, axis)
    upper = jnp.where(at == extent - 1, 2.0 * value - preceding, following)
    lower = jnp.where(at == 0, 2.0 * value - following, preceding)
    return (upper - lower) * 0.5


def cross(a, b):
    return [
        a[1] * b[2] - a[2] * b[1],
        a[2] * b[0] - a[0] * b[2],
        a[0] * b[1] - a[1] * b[0],
    ]


def metrics_kernel(own, halo, n_ref, disp_hbm, metrics_hbm, disp, ends, metrics, sems):
    space = lax.axis_index("space")
    copies = []

    def leave(source, target):
        copy = pltpu.make_async_copy(source, target, sems.at[len(copies)])
        copy.start()
        copies.append(copy)

    def strip_rows(strip, carry):
        rows = pl.ds(pl.multiple_of(strip * 8, 8), 8)
        for c in range(3):
            for half in range(2):
                lanes = slice(half * 128, half * 128 + 128)
                for p in range(2):
                    at = c * 32 + p * 16 + half * 8
                    disp[c, p, rows, lanes] = own[strip, at : at + 8, :]
                    at = c * 16 + half * 8
                    ends[p, c, rows, lanes] = halo[p, strip, at : at + 8, :]
        return carry

    lax.fori_loop(0, INST, strip_rows, 0, unroll=True)
    leave(disp, disp_hbm.at[0])

    for p in range(2):
        here = [n_ref[c, p] + disp[c, p] for c in range(3)]
        there = [n_ref[c, 1 - p] + disp[c, 1 - p] for c in range(3)]
        along_i = []
        for c in range(3):
            if p == 0:
                beyond = jnp.where(space == 0, 2.0 * here[c] - there[c], ends[0, c])
                along_i.append((there[c] - beyond) * 0.5)
            else:
                beyond = jnp.where(space == SPACE - 1, 2.0 * here[c] - there[c], ends[1, c])
                along_i.append((beyond - there[c]) * 0.5)
        along_j = [shifted(value, 0) for value in here]
        along_k = [shifted(value, 1) for value in here]
        one = cross(along_j, along_k)
        two = cross(along_k, along_i)
        three = cross(along_i, along_j)
        last = along_i[0] * one[0] + along_i[1] * one[1] + along_i[2] * one[2]
        row = 0
        for group in (one, two, three, [last]):
            for k, value in enumerate(group):
                metrics[p, row + k] = value
            rows = pl.ds(row, len(group))
            leave(metrics.at[p, rows], metrics_hbm.at[0, rows, p])
            row += len(group)
    for copy in copies:
        copy.wait()


def metric_rows(own, halo, base_nodes):
    anywhere = pl.BlockSpec(memory_space=pltpu.HBM)
    return pl.pallas_call(
        metrics_kernel,
        out_shape=(
            jax.ShapeDtypeStruct((1,) + base_nodes.shape, jnp.float32),
            jax.ShapeDtypeStruct((1, 10) + base_nodes.shape[1:], jnp.float32),
        ),
        in_specs=[vmem()] * 3,
        out_specs=(anywhere, anywhere),
        scratch_shapes=[
            pltpu.VMEM(base_nodes.shape, jnp.float32),
            pltpu.VMEM((2, 3) + base_nodes.shape[2:], jnp.float32),
            pltpu.VMEM((2, 10) + base_nodes.shape[2:], jnp.float32),
            pltpu.SemaphoreType.DMA((9,)),
        ],
        compiler_params=params(),
        name="metrics",
    )(own, halo, base_nodes)


def body(amplitudes, modal_coeffs, centre_positions, base_nodes):
    modes = amplitudes.shape[1]
    own = jnp.concatenate(
        [
            modal_coeffs.transpose(1, 2, 0).reshape(3 * OWN, modes),
            amplitudes,
            jnp.pad(centre_positions, ((0, 5), (0, modes - OWN))),
        ],
        axis=0,
    )
    gathered = gather(own)
    *placed, nodes = evaluate(gathered, base_nodes)
    own, halo = exchange(*placed, nodes)
    return metric_rows(own, halo, nodes)


def solution(mesh):
    in_specs = (
        P(),
        P(None, None, ("inst", "space")),
        P(None, ("inst", "space")),
        P(None, "space", None, None),
    )
    out_specs = (P("inst", None, "space", None, None), P("inst", None, "space", None, None))
    return jax.shard_map(body, mesh=mesh, in_specs=in_specs, out_specs=out_specs, check_vma=False)
```

```python
import jax
import jax.numpy as jnp
from jax import lax
from jax.experimental import pallas as pl
from jax.experimental.pallas import tpu as pltpu
from jax.sharding import PartitionSpec as P

MESH = pl.DeviceIdType.MESH
HIGH = lax.Precision.HIGHEST
XS, YS, ZS, CORES = 4, 4, 16, 2
INST, SPACE = YS * CORES, XS * ZS
OWN = 8
BLOCKS = XS * YS * CORES
NC = BLOCKS * ZS * OWN
VALUES = 32
BINS = 32
CHUNK = 128
GROUP = 8
REACH = 4
PLACED = 256
GROUPS = (NC + PLACED) // 32
MARGIN = 1.0 + 2.0**-11
VMEM_LIMIT = 32 * 1024 * 1024


def vmem():
    return pl.BlockSpec(memory_space=pltpu.VMEM)


def params(**more):
    return pltpu.CompilerParams(vmem_limit_bytes=VMEM_LIMIT, **more)


def swap_blocks(arrays):
    block = lax.broadcasted_iota(jnp.int32, arrays[0].shape, 1) // 16
    arrays = list(arrays)
    for step in (1, 2, 4):
        upper = (block & step) != 0
        for a in range(8):
            if not a & step:
                one, two = arrays[a], arrays[a | step]
                arrays[a] = jnp.where(upper, pltpu.roll(two, 16 * step, 1), one)
                arrays[a | step] = jnp.where(upper, two, pltpu.roll(one, 128 - 16 * step, 1))
    return arrays


def gather_kernel(own_ref, out_ref, zbuf, send, recv):
    inst, space = lax.axis_index("inst"), lax.axis_index("space")
    y, core = inst // CORES, inst % CORES
    x, z = space // ZS, space % ZS

    def along_z(d):
        return inst, x * ZS + lax.rem(z + (d + ZS), ZS)

    z_steps = [side * d for d in range(REACH, 0, -1) for side in (1, -1)]
    steps = [(a, b) for a in range(YS) for b in range(XS) if a or b]
    plane_peers = [
        (lax.rem(y + a, YS) * CORES + core, lax.rem(x + b, XS) * ZS + z) for a, b in steps
    ]
    other = (y * CORES + (1 - core), space)

    def hops(a, b):
        return min(a, YS - a) + min(b, XS - b)

    plane_order = sorted(range(len(steps)), key=lambda k: -hops(*steps[k]))
    peers = [along_z(d) for d in z_steps] + [plane_peers[k] for k in plane_order] + [other]
    barrier = pltpu.get_barrier_semaphore()
    for peer in peers:
        pl.semaphore_signal(barrier, inc=1, device_id=peer, device_id_type=MESH)

    transposed = (((1,), (1,)), ((), ()))

    def high_dot(a, b):
        return lax.dot_general(a, b, transposed, precision=HIGH, preferred_element_type=jnp.float32)

    amp = own_ref[24:32]
    eye = (
        lax.broadcasted_iota(jnp.int32, (OWN, OWN), 0) == lax.broadcasted_iota(jnp.int32, (OWN, OWN), 1)
    ).astype(jnp.float32)
    own = [high_dot(own_ref[8 * c : 8 * c + 8], amp) for c in range(3)]
    own.append(high_dot(eye, own_ref[32:40, 0:OWN])[:, 0:3])
    own = jnp.concatenate(own + [jnp.zeros((OWN, 128 - 27), jnp.float32)], axis=1)
    row_id = lax.broadcasted_iota(jnp.int32, (OWN, 128), 0) % 4
    spread = jnp.zeros((OWN, 128), jnp.float32)
    for a in range(4):
        moved = own if a == 0 else pltpu.roll(own, VALUES * a, 1)
        spread = spread + jnp.where(row_id == a, moved, 0.0)
    zbuf[z] = jnp.concatenate(
        [
            jnp.sum(spread[0:4], axis=0, keepdims=True),
            jnp.sum(spread[4:8], axis=0, keepdims=True),
        ],
        axis=0,
    )

    pl.semaphore_wait(barrier, len(peers))

    def start(ref, k, peer):
        copy = pltpu.make_async_remote_copy(
            src_ref=ref,
            dst_ref=ref,
            send_sem=send.at[k],
            recv_sem=recv.at[k],
            device_id=peer,
            device_id_type=MESH,
        )
        copy.start()
        return copy

    copies = [start(zbuf.at[z], k, along_z(d)) for k, d in enumerate(z_steps)]
    passed = []
    for d, copy in reversed(list(zip(z_steps, copies))):
        copy.wait_recv()
        if d < REACH:
            block = zbuf.at[lax.rem(z + (ZS - d), ZS)]
            passed.append(start(block, len(copies) + len(passed), along_z(REACH if d > 0 else -REACH)))
    for copy in copies:
        copy.wait_send()
    for copy in passed:
        copy.wait()
    rows = jnp.concatenate([zbuf[i] for i in range(ZS)], axis=0)
    rows = jnp.concatenate([rows, jnp.zeros((128 - 2 * ZS, 128), jnp.float32)], axis=0).T
    block = rows[0:VALUES]
    for a in range(1, 4):
        block = block + pltpu.roll(rows[VALUES * a : VALUES * (a + 1)], VALUES * a, 1)
    mine = core * (XS * YS) + y * XS + x
    out_ref[mine] = block

    copies = [start(out_ref.at[mine], ZS - 1 + k, plane_peers[k]) for k in plane_order]
    passed = [start(out_ref.at[mine], ZS - 1 + len(steps), other)]
    for copy, k in reversed(list(zip(copies, plane_order))):
        copy.wait_recv()
        a, b = steps[k]
        origin = core * (XS * YS) + lax.rem(y + YS - a, YS) * XS + lax.rem(x + XS - b, XS)
        passed.append(start(out_ref.at[origin], ZS + len(steps) + k, other))
    for copy in copies:
        copy.wait_send()
    for copy in passed:
        copy.wait()


def gather(own):
    count = ZS + 2 * XS * YS - 2
    return pl.pallas_call(
        gather_kernel,
        out_shape=jax.ShapeDtypeStruct((BLOCKS, VALUES, 128), jnp.float32),
        in_specs=[vmem()],
        out_specs=vmem(),
        scratch_shapes=[
            pltpu.VMEM((ZS, 2, 128), jnp.float32),
            pltpu.SemaphoreType.DMA((count,)),
            pltpu.SemaphoreType.DMA((count,)),
        ],
        compiler_params=params(collective_id=0, has_side_effects=True),
        cost_estimate=pl.CostEstimate(flops=10**9, bytes_accessed=2 * 10**7, transcendentals=0),
        name="gather",
    )(own)


def whole_dot(a, b, precision=None):
    return jnp.dot(a, b, precision=precision, preferred_element_type=jnp.float32)


def window(tiles, centres, windows, t, place):
    spot = [
        jnp.concatenate([centres[c * GROUPS + place + k] for k in range(4)], axis=0) for c in range(3)
    ]
    pieces = windows[place]
    tops, rests = [], []
    for p in range(2):
        square = None
        for c in range(3):
            gap = spot[c] - tiles[t, 2 * c + p : 2 * c + p + 1, :]
            square = gap * gap if square is None else square + gap * gap
        radius = square * lax.rsqrt(jnp.maximum(square, 1e-30))
        rest = jnp.maximum(1.0 - radius, 0.0)
        rest = rest * rest
        value = rest * rest * (4.0 * radius + 1.0)
        top = value.astype(jnp.bfloat16)
        tops.append(top)
        rests.append((value - top.astype(jnp.float32)).astype(jnp.bfloat16))
    full = whole_dot(pieces, jnp.concatenate(tops, axis=1))
    extra = whole_dot(pieces[0:32], jnp.concatenate(rests, axis=1))
    return full[0:24] + (full[24:48] + extra[0:24])


def evaluate_kernel(g_ref, n_ref, windows, centres, tiles, found, edges, kept, nodes, parts, order, weights, ends, arrived, passing):
    keep = pltpu.make_async_copy(n_ref, kept, passing)
    keep.start()
    first = pl.multiple_of(lax.axis_index("inst") * 8, 8)
    nodes[...] = n_ref[:, :, pl.ds(first, 8), :] * 0.25

    for half in range(2):
        lanes = slice(half * 128, half * 128 + 128)
        rows = [
            jnp.concatenate(
                [nodes[c, p, j : j + 1, lanes] for c in range(3) for p in range(2)]
                + [jnp.zeros((2, 128), jnp.float32)],
                axis=0,
            )
            for j in range(8)
        ]
        for t, tile in enumerate(swap_blocks(rows)):
            tiles[8 * half + t] = tile
    spots = [g_ref[:, 24 + c, :] * 0.25 for c in range(3)]
    near = None
    for c in range(3):
        low = jnp.min(nodes[c]) - MARGIN
        high = jnp.max(nodes[c]) + MARGIN
        inside = (spots[c] >= low) & (spots[c] <= high)
        near = inside if near is None else near & inside
        if c == 2:
            k_low, scale = low, BINS / jnp.full((1, 1), high - low)

    def bin_of(value):
        return jnp.clip(jnp.floor((value - k_low) * scale), 0.0, BINS - 1.0)

    bins = jnp.where(near, bin_of(spots[2]), -1.0)

    bin_id = lax.broadcasted_iota(jnp.int32, (BINS, 128), 0).astype(jnp.float32)
    member = jnp.concatenate(
        [(bins[i : i + 1] == bin_id).astype(jnp.float32) for i in range(BLOCKS)], axis=0
    )
    lane = lax.broadcasted_iota(jnp.int32, (128, 256), 1)
    counting = ((lax.broadcasted_iota(jnp.int32, (128, 256), 0) <= lane) | (lane >= 128)).astype(jnp.float32)
    counts = whole_dot(member.astype(jnp.bfloat16), counting.astype(jnp.bfloat16))
    total = counts[0:BINS, 128:256]
    for i in range(1, BLOCKS):
        total = total + counts[i * BINS : (i + 1) * BINS, 128:256]
    earlier = (
        lax.broadcasted_iota(jnp.int32, (BINS, BINS), 1) < lax.broadcasted_iota(jnp.int32, (BINS, BINS), 0)
    ).astype(jnp.float32)
    running = whole_dot(earlier, total, HIGH)
    rows = []
    for i in range(BLOCKS):
        own = slice(i * BINS, (i + 1) * BINS)
        rows.append(jnp.sum(member[own] * (running + counts[own, 0:128]), axis=0, keepdims=True) - 1.0)
        running = running + counts[own, 128:256]
    position = jnp.concatenate(rows + [jnp.zeros((128 - BLOCKS, 128), jnp.float32)], axis=0).T
    for i in range(BLOCKS):
        order[i * 128 : i * 128 + 128, :] = jnp.broadcast_to(position[:, i : i + 1], (128, 128))

    k_min = jnp.min(jnp.min(nodes[2], axis=0), axis=0, keepdims=True)
    k_max = jnp.max(jnp.max(nodes[2], axis=0), axis=0, keepdims=True)
    for step in (1, 2, 4, 8):
        k_min = jnp.minimum(k_min, pltpu.roll(k_min, step, 1))
        k_max = jnp.maximum(k_max, pltpu.roll(k_max, step, 1))
    wide_id = lax.broadcasted_iota(jnp.int32, (BINS, 256), 0).astype(jnp.float32)
    wide_total = jnp.concatenate([total, total], axis=1)
    start = jnp.sum(jnp.where(wide_id < bin_of(k_min - MARGIN), wide_total, 0.0), axis=0, keepdims=True)
    stop = jnp.sum(jnp.where(wide_id <= bin_of(k_max + MARGIN), wide_total, 0.0), axis=0, keepdims=True)
    begin = jnp.floor(start * (1.0 / 32.0))
    count = jnp.floor((jnp.maximum(stop - 32.0 * begin, 1.0) + (CHUNK - 1.0)) * (1.0 / CHUNK))
    edges[0:1, :] = begin.astype(jnp.int32)
    edges[1:2, :] = count.astype(jnp.int32)
    at_tile = lax.broadcasted_iota(jnp.int32, (1, 256), 1) % 16 == 15
    more = at_tile & (count > 1.0)
    tile_id = lax.broadcasted_iota(jnp.int32, (1, 256), 1) // 16
    lowest = jnp.min(jnp.where(more, tile_id, 16), axis=1, keepdims=True)
    highest = jnp.max(jnp.where(more, tile_id + 1, 0), axis=1, keepdims=True)
    edges[2:3, :] = jnp.broadcast_to(lowest, (1, 256))
    edges[3:4, :] = jnp.broadcast_to(highest, (1, 256))
    copy = pltpu.make_async_copy(edges, ends, arrived)
    copy.start()
    chunks = (jnp.sum(total[:, 0:1]).astype(jnp.int32) + (PLACED - 1)) // PLACED

    def split(i, carry):
        for half in range(2):
            value = g_ref[2 * i + half]
            motion = value[0:24]
            top = motion.astype(jnp.bfloat16).astype(jnp.float32)
            spot = value[24:32] * 0.25
            one = spot.astype(jnp.bfloat16).astype(jnp.float32)
            two = (spot - one).astype(jnp.bfloat16).astype(jnp.float32)
            three = spot - one - two
            parts[i, :, half * 128 : half * 128 + 128] = jnp.concatenate(
                [top, motion - top, one, two, three, jnp.zeros((8, 128), jnp.float32)], axis=0
            ).astype(jnp.bfloat16)
        return carry

    lax.fori_loop(0, BLOCKS // 2, split, 0)

    slot = lax.broadcasted_iota(jnp.int32, (1, 128), 1)

    def place_chunk(s, carry):
        sums = jnp.zeros((80, PLACED), jnp.float32)
        wanted = [(slot + (s * PLACED + 128 * half)).astype(jnp.float32) for half in range(2)]
        for i in range(BLOCKS // 2):
            at = order[i * 256 : i * 256 + 256, :]
            hit = jnp.concatenate([jnp.where(at == w, 1.0, 0.0) for w in wanted], axis=1)
            sums = sums + whole_dot(parts[i], hit.astype(jnp.bfloat16))
        short = sums[0:48]
        spot = (sums[48:56] + sums[56:64]) + sums[64:72]
        for half in range(2):
            lanes = slice(half * 128, half * 128 + 128)
            weights[2 * s + half] = short[:, lanes]
            piece = jnp.concatenate([spot[:, lanes], jnp.zeros((120, 128), jnp.float32)], axis=0).T
            for c in range(3):
                into = pl.ds(c * GROUPS + s * 8 + half * 4, 4)
                centres[into] = jnp.broadcast_to(piece[:, c : c + 1], (128, 128)).reshape(4, 32, 128)
        return carry

    lax.fori_loop(0, chunks, place_chunk, 0)

    behind = 2 * chunks
    for half in range(2):
        weights[behind + half] = jnp.zeros((48, CHUNK), jnp.float32)
        for c in range(3):
            centres[pl.ds(c * GROUPS + 4 * (behind + half), 4)] = jnp.zeros((4, 32, 128), jnp.float32)
    lane = lax.broadcasted_iota(jnp.int32, (48, CHUNK), 1)

    def shift_chunks(s, carry):
        values = [weights[2 * s + k] for k in range(3)]
        for k in range(2):
            place = 4 * (2 * s + k)
            windows[place] = values[k].astype(jnp.bfloat16)
            for r in range(1, 4):
                back = CHUNK - 32 * r
                moved = jnp.where(lane < back, pltpu.roll(values[k], back, 1), pltpu.roll(values[k + 1], back, 1))
                windows[place + r] = moved.astype(jnp.bfloat16)
        return carry

    lax.fori_loop(0, chunks, shift_chunks, 0)
    for r in range(4):
        windows[4 * behind + r] = jnp.zeros((48, CHUNK), jnp.bfloat16)

    found[...] = jnp.zeros_like(found)
    copy.wait()

    def more_windows(t, carry):
        def one(k, carry):
            found[t] += window(tiles, centres, windows, t, ends[0, 16 * t + 15] + 4 * k)
            return carry

        return lax.fori_loop(1, ends[1, 16 * t + 15], one, carry)

    lax.fori_loop(ends[2, 0], ends[3, 0], more_windows, 0)
    keep.wait()


def evaluate(gathered, base_nodes):
    shape = jax.ShapeDtypeStruct
    return pl.pallas_call(
        evaluate_kernel,
        out_shape=(
            shape((4 * (NC // CHUNK + 1), 48, CHUNK), jnp.bfloat16),
            shape((3 * GROUPS, 32, 128), jnp.float32),
            shape((16, 8, 128), jnp.float32),
            shape((16, 24, 256), jnp.float32),
            shape((8, 256), jnp.int32),
            shape(base_nodes.shape, jnp.float32),
        ),
        in_specs=[vmem()] * 2,
        out_specs=(vmem(),) * 6,
        scratch_shapes=[
            pltpu.VMEM((3, 2, 8, 256), jnp.float32),
            pltpu.VMEM((BLOCKS // 2, 80, 256), jnp.bfloat16),
            pltpu.VMEM((NC, 128), jnp.float32),
            pltpu.VMEM((NC // CHUNK + 2, 48, CHUNK), jnp.float32),
            pltpu.SMEM((8, 256), jnp.int32),
            pltpu.SemaphoreType.DMA,
            pltpu.SemaphoreType.DMA,
        ],
        compiler_params=params(),
        name="evaluate",
    )(gathered, base_nodes)


def exchange_kernel(windows, centres, tiles, more, edges, n_ref, own, halo, found, moved, deformed, send, recv, send_on, recv_on):
    inst, space = lax.axis_index("inst"), lax.axis_index("space")
    behind, ahead = lax.rem(space + SPACE - 1, SPACE), lax.rem(space + 1, SPACE)
    y, core = inst // CORES, inst % CORES

    def device(a, other):
        return lax.rem(y + a, YS) * CORES + (1 - core if other else core)

    order = [(0, 1)] + [(a, other) for a in (1, YS - 1, 2) for other in (0, 1)]
    peers = [(device(*step), space) for step in order] + [(inst, behind), (inst, ahead)]
    barrier = pltpu.get_barrier_semaphore()
    for peer in peers:
        pl.semaphore_signal(barrier, inc=1, device_id=peer, device_id_type=MESH)

    def start(source, target, sent, arrived, device):
        copy = pltpu.make_async_remote_copy(
            src_ref=source,
            dst_ref=target,
            send_sem=sent,
            recv_sem=arrived,
            device_id=device,
            device_id_type=MESH,
        )
        copy.start()
        return copy

    def first_windows(group, carry):
        for k in range(GROUP):
            t = group * GROUP + k
            found[t] = more[t] + window(tiles, centres, windows, t, edges[0, 16 * t + 15])
        return carry

    lax.fori_loop(0, 16 // GROUP, first_windows, 0)
    for p in range(2):
        for half in range(2):
            rows = swap_blocks([found[8 * half + t, :, p * 128 : p * 128 + 128] for t in range(8)])
            for j in range(8):
                for c in range(3):
                    into = pl.ds(c * 32 + p * 16 + half * 8 + j, 8, stride=96)
                    moved[into, :] = rows[j][c * 8 : c * 8 + 8]

    def add_nodes(strip):
        rows = pl.ds(pl.multiple_of(strip * 8, 8), 8)
        for c in range(3):
            for p in range(2):
                nodes = n_ref[c, p, rows, :]
                for half in range(2):
                    at, to = c * 32 + p * 16 + half * 8, c * 16 + half * 8
                    lanes = slice(half * 128, half * 128 + 128)
                    deformed[p, strip, to : to + 8, :] = own[strip, at : at + 8, :] + nodes[:, lanes]

    def pass_on(k, chip):
        strips = pl.ds(CORES * chip, CORES)
        return [
            start(
                deformed.at[side, strips],
                halo.at[1 - side, strips],
                send_on.at[side, k],
                recv_on.at[side, k],
                (inst, (behind, ahead)[side]),
            )
            for side in range(2)
        ]

    def rows_for(target):
        return pl.ds(pl.multiple_of(target * 96, 96), 96)

    own[inst] = moved[rows_for(inst), :]
    add_nodes(inst)
    pl.semaphore_wait(barrier, len(peers))
    copies = [
        start(moved.at[rows_for(peer[0])], own.at[inst], send.at[k], recv.at[k], peer)
        for k, peer in enumerate(peers[: len(order)])
    ]
    passed = []
    for k, a in enumerate((0, 1, YS - 1, 2)):
        for copy, step in zip(copies, order):
            if step[0] == a:
                copy.wait_recv()
                add_nodes(device(YS - a, step[1]))
        passed += pass_on(k, lax.rem(y + YS - a, YS))
    for copy in copies:
        copy.wait_send()
    for copy in passed:
        copy.wait()


def exchange(*arrays):
    return pl.pallas_call(
        exchange_kernel,
        out_shape=(
            jax.ShapeDtypeStruct((INST, 96, 128), jnp.float32),
            jax.ShapeDtypeStruct((2, INST, 48, 128), jnp.float32),
        ),
        in_specs=[vmem()] * 4 + [pl.BlockSpec(memory_space=pltpu.SMEM), vmem()],
        out_specs=(vmem(), vmem()),
        scratch_shapes=[
            pltpu.VMEM((16, 24, 256), jnp.float32),
            pltpu.VMEM((INST * 96, 128), jnp.float32),
            pltpu.VMEM((2, INST, 48, 128), jnp.float32),
            pltpu.SemaphoreType.DMA((INST,)),
            pltpu.SemaphoreType.DMA((INST,)),
            pltpu.SemaphoreType.DMA((2, YS)),
            pltpu.SemaphoreType.DMA((2, YS)),
        ],
        compiler_params=params(collective_id=1, has_side_effects=True),
        name="exchange",
    )(*arrays)


def shifted(value, axis):
    extent = value.shape[axis]
    at = lax.broadcasted_iota(jnp.int32, value.shape, axis)
    following = pltpu.roll(value, extent - 1, axis)
    preceding = pltpu.roll(value, 1, axis)
    upper = jnp.where(at == extent - 1, 2.0 * value - preceding, following)
    lower = jnp.where(at == 0, 2.0 * value - following, preceding)
    return (upper - lower) * 0.5


def cross(a, b):
    return [
        a[1] * b[2] - a[2] * b[1],
        a[2] * b[0] - a[0] * b[2],
        a[0] * b[1] - a[1] * b[0],
    ]


def metrics_kernel(own, halo, n_ref, disp_hbm, metrics_hbm, disp, ends, metrics, sems):
    space = lax.axis_index("space")
    copies = []

    def leave(source, target):
        copy = pltpu.make_async_copy(source, target, sems.at[len(copies)])
        copy.start()
        copies.append(copy)

    def strip_rows(strip, carry):
        rows = pl.ds(pl.multiple_of(strip * 8, 8), 8)
        for c in range(3):
            for half in range(2):
                lanes = slice(half * 128, half * 128 + 128)
                for p in range(2):
                    at = c * 32 + p * 16 + half * 8
                    disp[c, p, rows, lanes] = own[strip, at : at + 8, :]
                    at = c * 16 + half * 8
                    ends[p, c, rows, lanes] = halo[p, strip, at : at + 8, :]
        return carry

    lax.fori_loop(0, INST, strip_rows, 0, unroll=True)
    leave(disp, disp_hbm.at[0])

    for p in range(2):
        here = [n_ref[c, p] + disp[c, p] for c in range(3)]
        there = [n_ref[c, 1 - p] + disp[c, 1 - p] for c in range(3)]
        along_i = []
        for c in range(3):
            if p == 0:
                beyond = jnp.where(space == 0, 2.0 * here[c] - there[c], ends[0, c])
                along_i.append((there[c] - beyond) * 0.5)
            else:
                beyond = jnp.where(space == SPACE - 1, 2.0 * here[c] - there[c], ends[1, c])
                along_i.append((beyond - there[c]) * 0.5)
        along_j = [shifted(value, 0) for value in here]
        along_k = [shifted(value, 1) for value in here]
        one = cross(along_j, along_k)
        two = cross(along_k, along_i)
        three = cross(along_i, along_j)
        last = along_i[0] * one[0] + along_i[1] * one[1] + along_i[2] * one[2]
        row = 0
        for group in (one, two, three, [last]):
            for k, value in enumerate(group):
                metrics[p, row + k] = value
            rows = pl.ds(row, len(group))
            leave(metrics.at[p, rows], metrics_hbm.at[0, rows, p])
            row += len(group)
    for copy in copies:
        copy.wait()


def metric_rows(own, halo, base_nodes):
    anywhere = pl.BlockSpec(memory_space=pltpu.HBM)
    return pl.pallas_call(
        metrics_kernel,
        out_shape=(
            jax.ShapeDtypeStruct((1,) + base_nodes.shape, jnp.float32),
            jax.ShapeDtypeStruct((1, 10) + base_nodes.shape[1:], jnp.float32),
        ),
        in_specs=[vmem()] * 3,
        out_specs=(anywhere, anywhere),
        scratch_shapes=[
            pltpu.VMEM(base_nodes.shape, jnp.float32),
            pltpu.VMEM((2, 3) + base_nodes.shape[2:], jnp.float32),
            pltpu.VMEM((2, 10) + base_nodes.shape[2:], jnp.float32),
            pltpu.SemaphoreType.DMA((9,)),
        ],
        compiler_params=params(),
        name="metrics",
    )(own, halo, base_nodes)


def body(amplitudes, modal_coeffs, centre_positions, base_nodes):
    modes = amplitudes.shape[1]
    own = jnp.concatenate(
        [
            modal_coeffs.transpose(1, 2, 0).reshape(3 * OWN, modes),
            amplitudes,
            jnp.pad(centre_positions, ((0, 5), (0, modes - OWN))),
        ],
        axis=0,
    )
    gathered = gather(own)
    *placed, nodes = evaluate(gathered, base_nodes)
    own, halo = exchange(*placed, nodes)
    return metric_rows(own, halo, nodes)


def solution(mesh):
    in_specs = (
        P(),
        P(None, None, ("inst", "space")),
        P(None, ("inst", "space")),
        P(None, "space", None, None),
    )
    out_specs = (P("inst", None, "space", None, None), P("inst", None, "space", None, None))
    return jax.shard_map(body, mesh=mesh, in_specs=in_specs, out_specs=out_specs, check_vma=False)
```
